256 devices in a mesh: bl: 8 (over z_lo, y), row: 32 (over z_hi, x, core).
Axes of the slice: x: 4, y: 4, z: 8 (z_hi: 4, z_lo: 2; z = z_hi * 2 + z_lo), core: 2. Of those that a mesh axis runs over, the one named last changes fastest.
Arguments:
- visibilities: float32 [8, 32, 8, 2, 768], P('bl', 'row'), may hold values from -6 to 6
- kernels: float32 [8, 32, 8, 2, 8, 768], P('bl', 'row'), may hold values from 0.1 to 1
- offsets: int32 [8, 32, 8, 2, 768], P('bl', 'row'), may hold values from 0 to 120
- counts: int32 [8, 32, 8], P('bl', 'row'), may hold values from 0 to 768, as said below
- slot_tiles: int32 [8, 32, 8], P('bl', 'row'), may hold values from 0 to 127, as said below
- taper: float32 [8192, 8192], P(('row', 'bl')), may hold values from 0.5 to 1.5
Outputs:
- image: float32 [2, 8192, 8192], P(None, ('row', 'bl'))
The draws below stay inside these ranges and needn't reach their ends.
Inputs may be any that keep to these rules, and one draw needn't show every extreme that they name: Slot s of a device holds its first counts visibilities; slot 0 of every device is full, and devices of the middle bands hold more. `slot_tiles`: tiles of a band are numbered tile row times 8192 / 128 plus tile column; the slots of one device name different tiles.
All inputs are finite; a program needn't handle non-finite values.
Results may differ from the reference program's by a relative error of at most 0.0001.
Values sent between devices are 32-bit elements; how exact they have to be, the bound alone decides.
No kernel may reach another device: no remote copies, remote signals or barrier semaphores. Data moves between devices by JAX's collectives and lax.ppermute only.
A program may use at most 128 MiB of HBM per device.

```python
import jax
import jax.numpy as jnp
from jax import lax

G = 8192
TILE = 128
SUP = 8
SLOTS = 8
CAP = 768
BAND = 256
N_BL = 8
N_ROW = 32


def draw_counts(key, part):
    band_index = jnp.arange(N_ROW, dtype=jnp.int32)[None, :, None]
    middle = jnp.abs(2 * band_index - N_ROW + 1) < N_ROW // 2
    ceiling = jnp.where(middle, CAP, CAP // 4)
    ceiling = jnp.broadcast_to(ceiling, (N_BL, N_ROW, SLOTS))
    drawn = jax.random.randint(key, (N_BL, N_ROW, SLOTS), 0, ceiling + 1)
    first_slot = jnp.arange(SLOTS, dtype=jnp.int32)[None, None, :] == 0
    return jnp.where(first_slot, CAP, drawn).astype(jnp.int32)


def draw_slot_tiles(key, part):
    tile_total = BAND // TILE * (G // TILE)
    device_keys = jax.random.split(key, N_BL * N_ROW)
    picked = jax.vmap(lambda single: jax.random.permutation(single, tile_total)[:SLOTS])(device_keys)
    return picked.reshape(N_BL, N_ROW, SLOTS).astype(jnp.int32)


def set_ends(entries, rng, low, high):
    place = [jax.random.randint(jax.random.fold_in(rng, axis), (), 0, length) for axis, length in enumerate(entries.shape)]
    widest = entries.shape.index(max(entries.shape))
    neighbour = place[:widest] + [(place[widest] + 1) % entries.shape[widest]] + place[widest + 1:]
    return entries.at[tuple(place)].set(low).at[tuple(neighbour)].set(high)


def steps_of(stream_key, extent, pieces, low, top_value):
    factor_of = 1.0
    for dim, blocks in pieces:
        steps = jax.random.uniform(jax.random.fold_in(jax.random.fold_in(stream_key, 6), dim), (blocks,), jnp.float32, low / len(pieces), top_value / len(pieces))
        factor_of = factor_of * jnp.repeat(jnp.exp(steps), extent[dim] // blocks).reshape((-1,) + (1,) * (len(extent) - 1 - dim))
    return factor_of


def scatter_about(own_key, extent, width, reach, cuts=(), kind=jnp.bfloat16):
    values = width * jax.random.normal(own_key, extent, jnp.float32)
    if cuts:
        values = values * steps_of(own_key, extent, cuts, -0.22, 0.18)
    return jnp.clip(values, -reach, reach).astype(kind)


def setup_inputs(seed: int = 0) -> dict:
    key_list = jax.random.split(jax.random.key(seed), 7)
    visibilities = scatter_about(key_list[0], (N_BL, N_ROW, SLOTS, 2, CAP), 1.0, 6.0, ((0, 8), (1, 32)), jnp.float32)
    kernels = jnp.clip(0.1 + 0.9 * jax.random.uniform(key_list[1], (N_BL, N_ROW, SLOTS, 2, SUP, CAP), jnp.float32) ** steps_of(key_list[1], (N_BL, N_ROW, SLOTS, 2, SUP, CAP), ((0, 8), (1, 32)), -0.2, 0.2), 0.1, 1.0)
    offsets = set_ends(jax.random.randint(key_list[2], (N_BL, N_ROW, SLOTS, 2, CAP), 0, TILE - SUP + 1), jax.random.fold_in(key_list[2], 1), 0, TILE - SUP).astype(jnp.int32)
    counts = draw_counts(jax.random.fold_in(key_list[6], 71), 0)
    slot_tiles = draw_slot_tiles(jax.random.fold_in(key_list[6], 71), 0)
    taper = jnp.clip(0.5 + 1.0 * jax.random.uniform(key_list[5], (G, G), jnp.float32) ** steps_of(key_list[5], (G, G), ((0, 256),), -0.2, 0.2), 0.5, 1.5)
    return {"visibilities": visibilities, "kernels": kernels, "offsets": offsets, "counts": counts, "slot_tiles": slot_tiles, "taper": taper}


precise = lax.Precision.HIGHEST


def spread(kernel, offset_cells, side):
    cell_index = jnp.arange(side, dtype=jnp.int32)
    spread_sum = jnp.zeros(offset_cells.shape + (side,), kernel.dtype)
    for offset in range(kernel.shape[1]):
        matches = cell_index[None, None, :] == (offset_cells[:, :, None] + offset)
        spread_sum = spread_sum + kernel[:, offset, :, None] * matches.astype(kernel.dtype)
    return spread_sum


def grid_tiles(visible, kernel, offset_cells, slot_counts):
    capacity = visible.shape[2]
    live_mask = (jnp.arange(capacity, dtype=jnp.int32)[None, :] < slot_counts[:, None]).astype(visible.dtype)
    weights_row = spread(kernel[:, 0], offset_cells[:, 0], TILE) * live_mask[:, :, None]
    weights_col = spread(kernel[:, 1], offset_cells[:, 1], TILE)
    weighted = jnp.concatenate([weights_row * visible[:, 0, :, None], weights_row * visible[:, 1, :, None]], axis=2)
    tile_grids = jnp.einsum("scu,scv->suv", weighted, weights_col, precision=precise)
    return tile_grids.reshape(visible.shape[0], 2, TILE, TILE)


def reference(visibilities, kernels, offsets, counts, slot_tiles, taper):
    tile_columns = G // TILE

    def add_device(device_index, uv_grid):
        group_index = device_index // N_ROW
        band_index = device_index % N_ROW
        tile_grids = grid_tiles(visibilities[group_index, band_index], kernels[group_index, band_index], offsets[group_index, band_index], counts[group_index, band_index])
        chosen = slot_tiles[group_index, band_index]

        def add_slot(slot_index, partial_value):
            tile_number = chosen[slot_index]
            first_row = (band_index * BAND + (tile_number // tile_columns) * TILE).astype(jnp.int32)
            first_col = ((tile_number % tile_columns) * TILE).astype(jnp.int32)
            corner = (jnp.int32(0), first_row, first_col)
            current = lax.dynamic_slice(partial_value, corner, (2, TILE, TILE))
            return lax.dynamic_update_slice(partial_value, current + tile_grids[slot_index], corner)

        return lax.fori_loop(0, SLOTS, add_slot, uv_grid)

    uv_grid = lax.fori_loop(0, N_BL * N_ROW, add_device, jnp.zeros((2, G, G), jnp.float32))
    tapered = uv_grid * taper[None]
    spectrum = jnp.fft.fft2(lax.complex(tapered[0], tapered[1])) / G
    return jnp.stack([jnp.real(spectrum).T, jnp.imag(spectrum).T])
```

```python
import math

import jax
import jax.numpy as jnp
import ml_dtypes
import numpy as np
from jax import lax
from jax.experimental import pallas as pl
from jax.experimental.pallas import tpu as pltpu
from jax.sharding import PartitionSpec as P

G = 8192
TILE = 128
SUP = 8
SLOTS = 8
CAP = 768
N_BL = 8
N_ROW = 32
BANDS = 2
STRIP = TILE // N_BL
COLS = G // TILE
F32 = jnp.float32
BF16 = jnp.bfloat16
NT = (((1,), (1,)), ((), ()))


def unit(length, phase):
    angle = 2.0 * np.pi * (np.asarray(phase, np.int64) % length) / length
    return np.cos(angle), np.sin(angle)


def real_form(cosine, sine):
    return np.block([[cosine, sine], [-sine, cosine]])


def halves(table):
    high = table.astype(ml_dtypes.bfloat16)
    low = (table - high.astype(np.float64)).astype(ml_dtypes.bfloat16)
    return high, low


def split(value):
    high = value.astype(BF16)
    low = (value - high.astype(F32)).astype(BF16)
    return high, low


def add(left, right):
    return (left[0] + right[0], left[1] + right[1])


def sub(left, right):
    return (left[0] - right[0], left[1] - right[1])


def dft4(a, b, c, d):
    s, t = add(a, c), sub(a, c)
    u, v = add(b, d), sub(b, d)
    w = (v[1], -v[0])
    return [add(s, u), add(t, w), sub(s, u), sub(t, w)]


def dft8(x):
    even = dft4(x[0], x[2], x[4], x[6])
    odd = dft4(x[1], x[3], x[5], x[7])
    r = math.sqrt(0.5)
    turned = [
        odd[0],
        ((odd[1][0] + odd[1][1]) * r, (odd[1][1] - odd[1][0]) * r),
        (odd[2][1], -odd[2][0]),
        ((odd[3][1] - odd[3][0]) * r, (odd[3][1] + odd[3][0]) * -r),
    ]
    return [add(e, o) for e, o in zip(even, turned)] + [sub(e, o) for e, o in zip(even, turned)]


def mul(x, cosine, sine):
    return (x[0] * cosine + x[1] * sine, x[1] * cosine - x[0] * sine)


def grid_kernel(counts, tiles, vis, taps, offs, out):
    sub_index = lax.broadcasted_iota(jnp.int32, (SUP, CAP), 0)
    lane = lax.broadcasted_iota(jnp.int32, (1, CAP), 1)

    def place(block, taken):
        pieces = [jnp.where(taken == x, block, 0.0) for x in range(TILE // SUP)]
        return jnp.concatenate(pieces, axis=0).astype(BF16)

    def rotated(s, axis):
        first = jnp.broadcast_to(offs[s, axis : axis + 1, :], (SUP, CAP))
        shift = first & (SUP - 1)
        value = taps[s, axis]
        for bit in (1, 2, 4):
            value = jnp.where((shift & bit) != 0, pltpu.roll(value, bit, 0), value)
        taken = (first >> 3) + jnp.where(sub_index < shift, 1, 0)
        return value, taken

    def one_slot(s, carry):
        live = lane < counts[s]
        value, taken = rotated(s, 0)
        lefts = [split(value * jnp.where(live, vis[s, p : p + 1, :], 0.0)) for p in range(2)]
        left = jnp.concatenate(
            [place(lefts[p][h].astype(F32), taken) for h in range(2) for p in range(2)], axis=0
        )
        value, taken = rotated(s, 1)
        rights = split(value)
        right = jnp.concatenate([place(rights[h].astype(F32), taken) for h in range(2)], axis=0)
        prod = lax.dot_general(left, right, NT, preferred_element_type=F32)
        tile = (prod[:256, :128] + prod[256:, :128]) + (prod[:256, 128:] + prod[256:, 128:])
        for p in range(2):
            for d in range(N_BL):
                start = p * TILE + d * STRIP
                out[d, pl.ds(s * 32 + p * STRIP, STRIP), :] = tile[start : start + STRIP]
        number = jnp.full((1, TILE), tiles[s], jnp.int32).astype(F32)
        for d in range(N_BL):
            out[d, pl.ds(256 + s, 1), :] = number
        return carry

    lax.fori_loop(0, SLOTS, one_slot, 0)


def grid_call(counts, tiles, vis, taps, offs):
    smem = pl.BlockSpec(memory_space=pltpu.SMEM)
    vmem = pl.BlockSpec(memory_space=pltpu.VMEM)
    return pl.pallas_call(
        grid_kernel,
        out_shape=jax.ShapeDtypeStruct((N_BL, 264, TILE), F32),
        in_specs=[smem, smem, vmem, vmem, vmem],
        out_specs=vmem,
        compiler_params=pltpu.CompilerParams(vmem_limit_bytes=40 << 20),
    )(counts, tiles, vis, taps, offs)


def column_kernel(
    parity, strips, taper_a, taper_b, tw, wh, wl, out,
    taper, cells, half, xh, xl, ob, number, place, sem_in, sem_out,
):
    par = parity[0]
    in_a = pltpu.make_async_copy(taper_a, taper.at[par], sem_in.at[0])
    in_b = pltpu.make_async_copy(taper_b, taper.at[1 - par], sem_in.at[1])
    in_a.start()
    in_b.start()
    number[...] = strips[:, 256:264, :].reshape(64, TILE).astype(jnp.int32)
    to_scalar = pltpu.make_async_copy(number, place, sem_in.at[2])
    to_scalar.start()
    cells[...] = jnp.zeros_like(cells)
    to_scalar.wait()

    def add_strip(step, carry):
        tile = place[step, 0]
        start = pl.multiple_of((step % SLOTS) * 32, 32)
        rows = strips[step // SLOTS, pl.ds(start, 32), :]
        cells[tile] = cells[tile] + rows
        return carry

    lax.fori_loop(0, 64, add_strip, 0, unroll=4)
    in_a.wait()
    in_b.wait()
    copies = []
    for tr in range(BANDS):
        for a0 in range(8):
            x = []
            for a1 in range(8):
                a = a1 * 8 + a0
                t = taper[tr, :, a * TILE : (a + 1) * TILE]
                x.append((cells[tr * COLS + a, 0:16] * t, cells[tr * COLS + a, 16:32] * t))
            for k0, y in enumerate(dft8(x)):
                if a0 * k0:
                    c, s = unit(64, a0 * k0)
                    y = mul(y, float(c), float(s))
                half[k0 * 8 + a0, 0:16] = y[0]
                half[k0 * 8 + a0, 16:32] = y[1]
        for k0 in range(8):
            x = [(half[k0 * 8 + a0, 0:16], half[k0 * 8 + a0, 16:32]) for a0 in range(8)]
            for k1, y in enumerate(dft8(x)):
                k = k0 + 8 * k1
                y = mul(y, tw[0, k : k + 1, :], tw[1, k : k + 1, :])
                for p in range(2):
                    high, low = split(y[p])
                    xh[tr, k * 16 : k * 16 + 16, p * TILE : (p + 1) * TILE] = high
                    xl[tr, k * 16 : k * 16 + 16, p * TILE : (p + 1) * TILE] = low
        for block in range(4):
            rows_h = xh[tr, block * 256 : (block + 1) * 256, :]
            rows_l = xl[tr, block * 256 : (block + 1) * 256, :]
            prod = lax.dot_general(wh[...], rows_h, NT, preferred_element_type=F32)
            prod += lax.dot_general(wl[...], rows_h, NT, preferred_element_type=F32)
            prod += lax.dot_general(wh[...], rows_l, NT, preferred_element_type=F32)
            kh = block // 2
            for p in range(2):
                for m in range(2):
                    row = (p * 2 + tr) * 4 + (block % 2) * 2 + m
                    ob[kh * 16 + row] = prod[p * TILE : (p + 1) * TILE, m * TILE : (m + 1) * TILE]
                    copy = pltpu.make_async_copy(
                        ob.at[kh * 16 + row], out.at[:, kh, row, :], sem_out.at[kh * 16 + row]
                    )
                    copy.start()
                    copies.append(copy)
    for copy in copies:
        copy.wait()


def column_tables():
    k = np.arange(COLS)[:, None]
    y = np.arange(TILE)[None, :]
    turn = np.stack(unit(G, k * y)).astype(np.float32)
    q = np.arange(TILE)[:, None]
    high, low = halves(real_form(*unit(TILE, q * y)))
    return turn, high, low


def column_call(parity, strips, taper_a, taper_b):
    smem = pl.BlockSpec(memory_space=pltpu.SMEM)
    vmem = pl.BlockSpec(memory_space=pltpu.VMEM)
    hbm = pl.BlockSpec(memory_space=pl.ANY)
    return pl.pallas_call(
        column_kernel,
        out_shape=jax.ShapeDtypeStruct((TILE, 2, 16, TILE), F32),
        in_specs=[smem, vmem, hbm, hbm, vmem, vmem, vmem],
        out_specs=hbm,
        scratch_shapes=[
            pltpu.VMEM((2, STRIP, G), F32),
            pltpu.VMEM((BANDS * COLS, 32, TILE), F32),
            pltpu.VMEM((64, 32, TILE), F32),
            pltpu.VMEM((BANDS, 1024, 256), BF16),
            pltpu.VMEM((BANDS, 1024, 256), BF16),
            pltpu.VMEM((32, TILE, TILE), F32),
            pltpu.VMEM((64, TILE), jnp.int32),
            pltpu.SMEM((64, TILE), jnp.int32),
            pltpu.SemaphoreType.DMA((3,)),
            pltpu.SemaphoreType.DMA((32,)),
        ],
        compiler_params=pltpu.CompilerParams(vmem_limit_bytes=40 << 20),
    )(parity, strips, taper_a, taper_b, *column_tables())


def row_kernel(arrived, w1h, w1l, tw, gh, gl, out, x, at, bh, bl, sem):
    copies = []
    for dl in range(4):
        for s in range(16):
            pt, mb = s // 4, s % 4
            copy = pltpu.make_async_copy(
                arrived.at[:, dl, s, :],
                x.at[dl, pl.ds(pt * 64, 64), pl.ds(mb * TILE, TILE)],
                sem.at[dl * 16 + s],
            )
            copy.start()
            copies.append(copy)
    for dl in range(4):
        for copy in copies[dl * 16 : dl * 16 + 16]:
            copy.wait()
        high, low = split(x[dl])
        prod = jnp.dot(w1h[...], high, preferred_element_type=F32)
        prod += jnp.dot(w1l[...], high, preferred_element_type=F32)
        prod += jnp.dot(w1h[...], low, preferred_element_type=F32)
        at[dl] = prod

    def radix(step, carry):
        mb, block = step // 8, step % 8
        rows = pl.ds(pl.multiple_of(block * 16, 16), 16)
        rows_im = pl.ds(pl.multiple_of(TILE + block * 16, 16), 16)
        lanes = pl.ds(pl.multiple_of(mb * TILE, TILE), TILE)
        parts = [
            mul((at[dl, rows, lanes], at[dl, rows_im, lanes]), tw[dl, 0, rows, :], tw[dl, 1, rows, :])
            for dl in range(4)
        ]
        to_rows = pl.ds(pl.multiple_of(mb * TILE + block * 16, 16), 16)
        for kb, y in enumerate(dft4(*parts)):
            for p in range(2):
                high, low = split(y[p])
                bh[kb, to_rows, p * TILE : (p + 1) * TILE] = high
                bl[kb, to_rows, p * TILE : (p + 1) * TILE] = low
        return carry

    lax.fori_loop(0, 32, radix, 0)
    for kb in range(4):
        prod = lax.dot_general(gh[kb], bh[kb], NT, preferred_element_type=F32)
        prod += lax.dot_general(gl[kb], bh[kb], NT, preferred_element_type=F32)
        prod += lax.dot_general(gh[kb], bl[kb], NT, preferred_element_type=F32)
        for p in range(2):
            for k2 in range(16):
                row = p * TILE + k2 * 8
                to = (k2 * 4 + kb) * TILE
                for mb in range(4):
                    out[p, mb * 8 : mb * 8 + 8, to : to + TILE] = prod[
                        row : row + 8, mb * TILE : (mb + 1) * TILE
                    ]


def row_tables():
    ka = np.arange(TILE)[:, None]
    tr, r, dh = np.meshgrid(np.arange(2), np.arange(N_ROW), np.arange(2), indexing="ij")
    coarse = (r * 4 + tr * 2 + dh).reshape(1, TILE)
    w1h, w1l = halves(real_form(*unit(TILE, ka * coarse)))
    fine = np.arange(TILE)[None, :] % 16
    turn = np.stack([np.stack(unit(G, ka * (dl * 16 + fine))) for dl in range(4)])
    k2, j = np.meshgrid(np.arange(16), np.arange(8), indexing="ij")
    k2, j = k2.reshape(TILE, 1), j.reshape(TILE, 1)
    jj, i = np.meshgrid(np.arange(8), np.arange(16), indexing="ij")
    jj, i = jj.reshape(1, TILE), i.reshape(1, TILE)
    same = (j == jj) / G
    last = []
    for kb in range(4):
        cosine, sine = unit(64, i * (kb + 4 * k2))
        last.append(real_form(cosine * same, sine * same))
    gh, gl = halves(np.stack(last))
    return w1h, w1l, turn.astype(np.float32), gh, gl


def row_call(arrived):
    vmem = pl.BlockSpec(memory_space=pltpu.VMEM)
    hbm = pl.BlockSpec(memory_space=pl.ANY)
    return pl.pallas_call(
        row_kernel,
        out_shape=jax.ShapeDtypeStruct((2, 32, G), F32),
        in_specs=[hbm, vmem, vmem, vmem, vmem, vmem],
        out_specs=vmem,
        scratch_shapes=[
            pltpu.VMEM((4, 256, 512), F32),
            pltpu.VMEM((4, 256, 512), F32),
            pltpu.VMEM((4, 512, 256), BF16),
            pltpu.VMEM((4, 512, 256), BF16),
            pltpu.SemaphoreType.DMA((64,)),
        ],
        compiler_params=pltpu.CompilerParams(vmem_limit_bytes=40 << 20),
    )(arrived, *row_tables())


def body(visibilities, kernels, offsets, counts, slot_tiles, taper):
    me = lax.axis_index("bl")
    low = me < N_BL // 2
    first = jnp.where(low, 0, STRIP)
    taper_a = lax.dynamic_slice(taper, (first, 0), (STRIP, G))
    taper_b = lax.dynamic_slice(taper, (STRIP - first, 0), (STRIP, G))
    to_a = [(s, (2 * s + (s >= 4)) % 8) for s in range(N_BL)]
    to_b = [(s, (2 * s + (s < 4)) % 8) for s in range(N_BL)]
    taper_a = lax.ppermute(taper_a, "bl", to_a)
    taper_b = lax.ppermute(taper_b, "bl", to_b)
    strips = grid_call(
        counts[0, 0], slot_tiles[0, 0], visibilities[0, 0], kernels[0, 0], offsets[0, 0]
    )
    strips = lax.all_to_all(strips, "bl", 0, 0, tiled=True)
    parity = (me % 2).reshape(1).astype(jnp.int32)
    leaving = column_call(parity, strips, taper_a, taper_b)
    arrived = lax.all_to_all(leaving.reshape(256, 16, TILE), ("row", "bl"), 0, 0, tiled=True)
    return row_call(arrived.reshape(64, 4, 16, TILE))


def solution(mesh):
    in_specs = (
        P("bl", "row", None, None, None),
        P("bl", "row", None, None, None, None),
        P("bl", "row", None, None, None),
        P("bl", "row", None),
        P("bl", "row", None),
        P(("row", "bl"), None),
    )
    out_specs = P(None, ("row", "bl"), None)
    return jax.shard_map(body, mesh=mesh, in_specs=in_specs, out_specs=out_specs, check_vma=False)
```

```python
import math

import jax
import jax.numpy as jnp
import ml_dtypes
import numpy as np
from jax import lax
from jax.experimental import pallas as pl
from jax.experimental.pallas import tpu as pltpu
from jax.sharding import PartitionSpec as P

G = 8192
TILE = 128
SUP = 8
SLOTS = 8
CAP = 768
N_BL = 8
N_ROW = 32
BANDS = 2
STRIP = TILE // N_BL
COLS = G // TILE
F32 = jnp.float32
BF16 = jnp.bfloat16
HBM = pltpu.MemorySpace.HBM
NT = (((1,), (1,)), ((), ()))


def unit(length, phase):
    angle = 2.0 * np.pi * (np.asarray(phase, np.int64) % length) / length
    return np.cos(angle), np.sin(angle)


def real_form(cosine, sine):
    return np.block([[cosine, sine], [-sine, cosine]])


def halves(table):
    high = table.astype(ml_dtypes.bfloat16)
    low = (table - high.astype(np.float64)).astype(ml_dtypes.bfloat16)
    return high, low


def split(value):
    high = value.astype(BF16)
    low = (value - high.astype(F32)).astype(BF16)
    return high, low


def add(left, right):
    return (left[0] + right[0], left[1] + right[1])


def sub(left, right):
    return (left[0] - right[0], left[1] - right[1])


def dft4(a, b, c, d):
    s, t = add(a, c), sub(a, c)
    u, v = add(b, d), sub(b, d)
    w = (v[1], -v[0])
    return [add(s, u), add(t, w), sub(s, u), sub(t, w)]


def dft8(x):
    even = dft4(x[0], x[2], x[4], x[6])
    odd = dft4(x[1], x[3], x[5], x[7])
    r = math.sqrt(0.5)
    turned = [
        odd[0],
        ((odd[1][0] + odd[1][1]) * r, (odd[1][1] - odd[1][0]) * r),
        (odd[2][1], -odd[2][0]),
        ((odd[3][1] - odd[3][0]) * r, (odd[3][1] + odd[3][0]) * -r),
    ]
    return [add(e, o) for e, o in zip(even, turned)] + [sub(e, o) for e, o in zip(even, turned)]


def mul(x, cosine, sine):
    return (x[0] * cosine + x[1] * sine, x[1] * cosine - x[0] * sine)


def grid_kernel(
    counts_in, tiles_in, vis_in, taps_in, offs_in, out,
    counts, tiles, vis, taps, offs, strips, number, sem_few, sem_in, sem_out, sem_num,
):
    few = [
        pltpu.make_async_copy(counts_in, counts, sem_few.at[0]),
        pltpu.make_async_copy(tiles_in, tiles, sem_few.at[1]),
        pltpu.make_async_copy(vis_in, vis, sem_few.at[2]),
        pltpu.make_async_copy(offs_in, offs, sem_few.at[3]),
    ]
    for copy in few:
        copy.start()
    tap_copies = []
    for s in range(SLOTS):
        copy = pltpu.make_async_copy(taps_in.at[s], taps.at[s], sem_in.at[s])
        copy.start()
        tap_copies.append(copy)
    for copy in few:
        copy.wait()
    sub_index = lax.broadcasted_iota(jnp.int32, (SUP, CAP), 0)
    lane = lax.broadcasted_iota(jnp.int32, (1, CAP), 1)
    slot_index = lax.broadcasted_iota(jnp.int32, (SLOTS, TILE), 0)
    numbers = jnp.zeros((SLOTS, TILE), jnp.int32)
    for s in range(SLOTS):
        numbers = jnp.where(slot_index == s, tiles[0, s], numbers)
    number[...] = numbers.astype(F32)
    leaving = []
    for d in range(N_BL):
        copy = pltpu.make_async_copy(number, out.at[d, pl.ds(256, 8), :], sem_num.at[d])
        copy.start()
        leaving.append(copy)

    def place(block, taken):
        pieces = [jnp.where(taken == x, block, 0.0) for x in range(TILE // SUP)]
        return jnp.concatenate(pieces, axis=0).astype(BF16)

    def rotated(s, axis):
        first = jnp.broadcast_to(offs[s, axis : axis + 1, :], (SUP, CAP))
        shift = first & (SUP - 1)
        value = taps[s, axis]
        for bit in (1, 2, 4):
            value = jnp.where((shift & bit) != 0, pltpu.roll(value, bit, 0), value)
        taken = (first >> 3) + jnp.where(sub_index < shift, 1, 0)
        return value, taken

    for s in range(SLOTS):
        tap_copies[s].wait()
        live = lane < counts[0, s]
        value, taken = rotated(s, 0)
        lefts = [split(value * jnp.where(live, vis[s, p : p + 1, :], 0.0)) for p in range(2)]
        left = jnp.concatenate(
            [place(lefts[p][h].astype(F32), taken) for h in range(2) for p in range(2)], axis=0
        )
        value, taken = rotated(s, 1)
        rights = split(value)
        right = jnp.concatenate([place(rights[h].astype(F32), taken) for h in range(2)], axis=0)
        prod = lax.dot_general(left, right, NT, preferred_element_type=F32)
        tile = (prod[:256, :128] + prod[256:, :128]) + (prod[:256, 128:] + prod[256:, 128:])
        for p in range(2):
            for d in range(N_BL):
                start = p * TILE + first_row(d)
                strips[s, d, p * STRIP : (p + 1) * STRIP, :] = tile[start : start + STRIP]
        copy = pltpu.make_async_copy(strips.at[s], out.at[:, pl.ds(s * 32, 32), :], sem_out.at[s])
        copy.start()
        leaving.append(copy)
    for copy in leaving:
        copy.wait()


def first_row(d):
    return (d % 4) * 32 + (d // 4) * STRIP


def grid_call(counts, tiles, vis, taps, offs):
    hbm = pl.BlockSpec(memory_space=HBM)
    return pl.pallas_call(
        grid_kernel,
        out_shape=jax.ShapeDtypeStruct((N_BL, 264, TILE), F32),
        in_specs=[hbm] * 5,
        out_specs=hbm,
        scratch_shapes=[
            pltpu.SMEM((1, SLOTS), jnp.int32),
            pltpu.SMEM((1, SLOTS), jnp.int32),
            pltpu.VMEM((SLOTS, 2, CAP), F32),
            pltpu.VMEM((SLOTS, 2, SUP, CAP), F32),
            pltpu.VMEM((SLOTS, 2, CAP), jnp.int32),
            pltpu.VMEM((SLOTS, N_BL, 32, TILE), F32),
            pltpu.VMEM((SLOTS, TILE), F32),
            pltpu.SemaphoreType.DMA((4,)),
            pltpu.SemaphoreType.DMA((SLOTS,)),
            pltpu.SemaphoreType.DMA((SLOTS,)),
            pltpu.SemaphoreType.DMA((N_BL,)),
        ],
        compiler_params=pltpu.CompilerParams(vmem_limit_bytes=60 << 20),
        cost_estimate=pl.CostEstimate(flops=4 << 30, bytes_accessed=8 << 20, transcendentals=0),
    )(counts, tiles, vis, taps, offs)


def column_kernel(
    side, strips, taper_own, taper_in, taper_more, tw, wh, wl, out,
    taper, cells, half, xh, xl, ob, number, place, sem_in,
):
    mine = side[0]
    kept = pl.ds(pl.multiple_of(mine * STRIP, STRIP), STRIP)
    in_a = pltpu.make_async_copy(taper_own.at[kept], taper.at[mine], sem_in.at[0])
    in_b = pltpu.make_async_copy(taper_in, taper.at[1 - mine, pl.ds(0, 8)], sem_in.at[1])
    in_c = pltpu.make_async_copy(taper_more, taper.at[1 - mine, pl.ds(8, 8)], sem_in.at[3])
    in_a.start()
    in_b.start()
    in_c.start()
    number[...] = strips[:, 256:264, :].reshape(64, TILE).astype(jnp.int32)
    to_scalar = pltpu.make_async_copy(number, place, sem_in.at[2])
    to_scalar.start()
    cells[...] = jnp.zeros_like(cells)
    to_scalar.wait()

    def add_strip(step, carry):
        tile = place[step, 0]
        start = pl.multiple_of((step % SLOTS) * 32, 32)
        rows = strips[step // SLOTS, pl.ds(start, 32), :]
        cells[tile] = cells[tile] + rows
        return carry

    lax.fori_loop(0, 64, add_strip, 0, unroll=4)
    in_a.wait()
    in_b.wait()
    in_c.wait()
    for tr in range(BANDS):
        for a0 in range(8):
            x = []
            for a1 in range(8):
                a = a1 * 8 + a0
                t = taper[tr, :, a * TILE : (a + 1) * TILE]
                x.append((cells[tr * COLS + a, 0:16] * t, cells[tr * COLS + a, 16:32] * t))
            for k0, y in enumerate(dft8(x)):
                if a0 * k0:
                    c, s = unit(64, a0 * k0)
                    y = mul(y, float(c), float(s))
                half[k0 * 8 + a0, 0:16] = y[0]
                half[k0 * 8 + a0, 16:32] = y[1]
        for k0 in range(8):
            x = [(half[k0 * 8 + a0, 0:16], half[k0 * 8 + a0, 16:32]) for a0 in range(8)]
            for k1, y in enumerate(dft8(x)):
                k = k0 + 8 * k1
                y = mul(y, tw[0, k : k + 1, :], tw[1, k : k + 1, :])
                for p in range(2):
                    high, low = split(y[p])
                    xh[tr, k * 16 : k * 16 + 16, p * TILE : (p + 1) * TILE] = high
                    xl[tr, k * 16 : k * 16 + 16, p * TILE : (p + 1) * TILE] = low
        for block in range(4):
            rows_h = xh[tr, block * 256 : (block + 1) * 256, :]
            rows_l = xl[tr, block * 256 : (block + 1) * 256, :]
            prod = lax.dot_general(wh[...], rows_h, NT, preferred_element_type=F32)
            prod += lax.dot_general(wl[...], rows_h, NT, preferred_element_type=F32)
            prod += lax.dot_general(wh[...], rows_l, NT, preferred_element_type=F32)
            kh = block // 2
            for p in range(2):
                for m in range(2):
                    row = tr * 4 + (block % 2) * 2 + m
                    ob[kh, p, row] = prod[p * TILE : (p + 1) * TILE, m * TILE : (m + 1) * TILE]
            if tr == 1 and block % 2 == 1:
                for p in range(2):
                    out[kh, :, p * 8 : p * 8 + 8, :] = jnp.swapaxes(ob[kh, p], 0, 1)


def column_tables():
    k = np.arange(COLS)[:, None]
    y = np.arange(TILE)[None, :]
    turn = np.stack(unit(G, k * y)).astype(np.float32)
    zl, r, yh = np.meshgrid(np.arange(2), np.arange(N_ROW), np.arange(2), indexing="ij")
    q = (r * 4 + zl * 2 + yh).reshape(TILE, 1)
    high, low = halves(real_form(*unit(TILE, q * y)))
    return turn, high, low


def column_call(side, strips, taper_own, taper_in, taper_more):
    smem = pl.BlockSpec(memory_space=pltpu.SMEM)
    vmem = pl.BlockSpec(memory_space=pltpu.VMEM)
    hbm = pl.BlockSpec(memory_space=pl.ANY)
    return pl.pallas_call(
        column_kernel,
        out_shape=jax.ShapeDtypeStruct((2, TILE, 16, TILE), F32),
        in_specs=[smem, vmem, hbm, hbm, hbm, vmem, vmem, vmem],
        out_specs=vmem,
        scratch_shapes=[
            pltpu.VMEM((2, STRIP, G), F32),
            pltpu.VMEM((BANDS * COLS, 32, TILE), F32),
            pltpu.VMEM((64, 32, TILE), F32),
            pltpu.VMEM((BANDS, 1024, 256), BF16),
            pltpu.VMEM((BANDS, 1024, 256), BF16),
            pltpu.VMEM((2, 2, 8, TILE, TILE), F32),
            pltpu.VMEM((64, TILE), jnp.int32),
            pltpu.SMEM((64, TILE), jnp.int32),
            pltpu.SemaphoreType.DMA((4,)),
        ],
        compiler_params=pltpu.CompilerParams(vmem_limit_bytes=40 << 20),
    )(side, strips, taper_own, taper_in, taper_more, *column_tables())


def row_kernel(arrived, w1h, w1l, tw, gh, gl, out, xh, xl, at, bh, bl):
    for dl in range(4):
        for half in range(2):
            rows = jnp.swapaxes(arrived[dl, :, half * 8 : half * 8 + 8, :], 0, 1)
            for t in range(8):
                to = (half * 2 + t // 4) * 64
                lanes = (t % 4) * TILE
                high, low = split(rows[t])
                xh[dl, to : to + 64, lanes : lanes + TILE] = high
                xl[dl, to : to + 64, lanes : lanes + TILE] = low
        prod = jnp.dot(w1h[...], xh[dl], preferred_element_type=F32)
        prod += jnp.dot(w1l[...], xh[dl], preferred_element_type=F32)
        prod += jnp.dot(w1h[...], xl[dl], preferred_element_type=F32)
        at[dl] = prod

    def radix(step, carry):
        mb, block = step // 8, step % 8
        rows = pl.ds(pl.multiple_of(block * 16, 16), 16)
        rows_im = pl.ds(pl.multiple_of(TILE + block * 16, 16), 16)
        lanes = pl.ds(pl.multiple_of(mb * TILE, TILE), TILE)
        parts = [
            mul((at[dl, rows, lanes], at[dl, rows_im, lanes]), tw[dl, 0, rows, :], tw[dl, 1, rows, :])
            for dl in range(4)
        ]
        to_rows = pl.ds(pl.multiple_of(mb * TILE + block * 16, 16), 16)
        for kb, y in enumerate(dft4(*parts)):
            for p in range(2):
                high, low = split(y[p])
                bh[kb, to_rows, p * TILE : (p + 1) * TILE] = high
                bl[kb, to_rows, p * TILE : (p + 1) * TILE] = low
        return carry

    lax.fori_loop(0, 32, radix, 0)
    for kb in range(4):
        prod = lax.dot_general(gh[kb], bh[kb], NT, preferred_element_type=F32)
        prod += lax.dot_general(gl[kb], bh[kb], NT, preferred_element_type=F32)
        prod += lax.dot_general(gh[kb], bl[kb], NT, preferred_element_type=F32)
        for p in range(2):
            for k2 in range(16):
                row = p * TILE + k2 * 8
                to = (k2 * 4 + kb) * TILE
                for mb in range(4):
                    out[p, mb * 8 : mb * 8 + 8, to : to + TILE] = prod[
                        row : row + 8, mb * TILE : (mb + 1) * TILE
                    ]


def row_tables():
    ka = np.arange(TILE)[:, None]
    tr, r, yh = np.meshgrid(np.arange(2), np.arange(N_ROW), np.arange(2), indexing="ij")
    coarse = (r * 4 + tr * 2 + yh).reshape(1, TILE)
    w1h, w1l = halves(real_form(*unit(TILE, ka * coarse)))
    fine = np.arange(TILE)[None, :] % 16
    turn = np.stack([np.stack(unit(G, ka * (dl * 16 + fine))) for dl in range(4)])
    k2, j = np.meshgrid(np.arange(16), np.arange(8), indexing="ij")
    k2, j = k2.reshape(TILE, 1), j.reshape(TILE, 1)
    jj, i = np.meshgrid(np.arange(8), np.arange(16), indexing="ij")
    jj, i = jj.reshape(1, TILE), i.reshape(1, TILE)
    same = (j == jj) / G
    last = []
    for kb in range(4):
        cosine, sine = unit(64, i * (kb + 4 * k2))
        last.append(real_form(cosine * same, sine * same))
    gh, gl = halves(np.stack(last))
    return w1h, w1l, turn.astype(np.float32), gh, gl


def row_call(arrived):
    vmem = pl.BlockSpec(memory_space=pltpu.VMEM)
    return pl.pallas_call(
        row_kernel,
        out_shape=jax.ShapeDtypeStruct((2, 32, G), F32),
        in_specs=[vmem, vmem, vmem, vmem, vmem, vmem],
        out_specs=vmem,
        scratch_shapes=[
            pltpu.VMEM((4, 256, 512), BF16),
            pltpu.VMEM((4, 256, 512), BF16),
            pltpu.VMEM((4, 256, 512), F32),
            pltpu.VMEM((4, 512, 256), BF16),
            pltpu.VMEM((4, 512, 256), BF16),
        ],
        compiler_params=pltpu.CompilerParams(vmem_limit_bytes=40 << 20),
    )(arrived, *row_tables())


def body(visibilities, kernels, offsets, counts, slot_tiles, taper):
    side = lax.axis_index("bl") // 4
    swap = [(s, (s + 4) % 8) for s in range(N_BL)]
    given = lax.dynamic_slice(taper, ((1 - side) * STRIP, 0), (8, G))
    taper_in = lax.ppermute(given, "bl", swap)
    strips = grid_call(counts[0], slot_tiles[0], visibilities[0, 0], kernels[0, 0], offsets[0, 0])
    strips, taper_in = lax.optimization_barrier((strips, taper_in))
    given = lax.dynamic_slice(taper, ((1 - side) * STRIP + 8, 0), (8, G))
    taper_more = lax.ppermute(given, "bl", swap)
    strips = lax.all_to_all(strips, "bl", 0, 0, tiled=True)
    side = side.reshape(1).astype(jnp.int32)
    leaving = column_call(side, strips, taper, taper_in, taper_more)
    arrived = lax.all_to_all(
        leaving.reshape(256, 16, TILE), ("bl", "row"), 0, 0, axis_index_groups=members(), tiled=True
    )
    return row_call(arrived.reshape(4, 64, 16, TILE))


def members():
    group = []
    for yl in range(2):
        for zl in range(2):
            for r in range(N_ROW):
                for yh in range(2):
                    group.append((zl * 4 + yh * 2 + yl) * N_ROW + r)
    return [group]


def solution(mesh):
    in_specs = (
        P("bl", "row", None, None, None),
        P("bl", "row", None, None, None, None),
        P("bl", "row", None, None, None),
        P("bl", "row", None),
        P("bl", "row", None),
        P(("row", "bl"), None),
    )
    out_specs = P(None, ("row", "bl"), None)
    return jax.shard_map(body, mesh=mesh, in_specs=in_specs, out_specs=out_specs, check_vma=False)
```

```python
import math

import jax
import jax.numpy as jnp
import ml_dtypes
import numpy as np
from jax import lax
from jax.experimental import pallas as pl
from jax.experimental.pallas import tpu as pltpu
from jax.sharding import PartitionSpec as P

G = 8192
TILE = 128
SUP = 8
SLOTS = 8
CAP = 768
N_BL = 8
N_ROW = 32
BANDS = 2
STRIP = TILE // N_BL
COLS = G // TILE
F32 = jnp.float32
BF16 = jnp.bfloat16
HBM = pltpu.MemorySpace.HBM
NT = (((1,), (1,)), ((), ()))


def unit(length, phase):
    angle = 2.0 * np.pi * (np.asarray(phase, np.int64) % length) / length
    return np.cos(angle), np.sin(angle)


def real_form(cosine, sine):
    return np.block([[cosine, sine], [-sine, cosine]])


def halves(table):
    high = table.astype(ml_dtypes.bfloat16)
    low = (table - high.astype(np.float64)).astype(ml_dtypes.bfloat16)
    return high, low


def split(value):
    high = value.astype(BF16)
    low = (value - high.astype(F32)).astype(BF16)
    return high, low


def add(left, right):
    return (left[0] + right[0], left[1] + right[1])


def sub(left, right):
    return (left[0] - right[0], left[1] - right[1])


def dft4(a, b, c, d):
    s, t = add(a, c), sub(a, c)
    u, v = add(b, d), sub(b, d)
    w = (v[1], -v[0])
    return [add(s, u), add(t, w), sub(s, u), sub(t, w)]


def dft8(x):
    even = dft4(x[0], x[2], x[4], x[6])
    odd = dft4(x[1], x[3], x[5], x[7])
    r = math.sqrt(0.5)
    turned = [
        odd[0],
        ((odd[1][0] + odd[1][1]) * r, (odd[1][1] - odd[1][0]) * r),
        (odd[2][1], -odd[2][0]),
        ((odd[3][1] - odd[3][0]) * r, (odd[3][1] + odd[3][0]) * -r),
    ]
    return [add(e, o) for e, o in zip(even, turned)] + [sub(e, o) for e, o in zip(even, turned)]


def mul(x, cosine, sine):
    return (x[0] * cosine + x[1] * sine, x[1] * cosine - x[0] * sine)


def grid_kernel(
    me, counts_in, tiles_in, vis_in, taps_in, offs_in,
    out0, out1, out2, out3, out4, out5, out6, out7,
    counts, tiles, vis, taps, offs, strips, sem_few, sem_in, sem_out,
):
    outs = [out0, out1, out2, out3, out4, out5, out6, out7]
    few = [
        pltpu.make_async_copy(counts_in, counts, sem_few.at[0]),
        pltpu.make_async_copy(tiles_in, tiles, sem_few.at[1]),
        pltpu.make_async_copy(vis_in, vis, sem_few.at[2]),
        pltpu.make_async_copy(offs_in, offs, sem_few.at[3]),
    ]
    for copy in few:
        copy.start()
    tap_copies = []
    for s in range(SLOTS):
        copy = pltpu.make_async_copy(taps_in.at[s], taps.at[s], sem_in.at[s])
        copy.start()
        tap_copies.append(copy)
    for copy in few:
        copy.wait()
    sub_index = lax.broadcasted_iota(jnp.int32, (SUP, CAP), 0)
    lane = lax.broadcasted_iota(jnp.int32, (1, CAP), 1)
    slot_index = lax.broadcasted_iota(jnp.int32, (SLOTS, TILE), 0)
    numbers = jnp.zeros((SLOTS, TILE), jnp.int32)
    for s in range(SLOTS):
        numbers = jnp.where(slot_index == s, tiles[0, s], numbers)
    for block in range(N_BL):
        strips[block, 32] = numbers.astype(F32)
    leaving = []

    def place(block, taken):
        pieces = [jnp.where(taken == x, block, 0.0) for x in range(TILE // SUP)]
        return jnp.concatenate(pieces, axis=0).astype(BF16)

    def rotated(s, axis):
        first = jnp.broadcast_to(offs[s, axis : axis + 1, :], (SUP, CAP))
        shift = first & (SUP - 1)
        value = taps[s, axis]
        for bit in (1, 2, 4):
            value = jnp.where((shift & bit) != 0, pltpu.roll(value, bit, 0), value)
        taken = (first >> 3) + jnp.where(sub_index < shift, 1, 0)
        return value, taken

    for s in range(SLOTS):
        tap_copies[s].wait()
        live = lane < counts[0, s]
        value, taken = rotated(s, 0)
        lefts = [split(value * jnp.where(live, vis[s, p : p + 1, :], 0.0)) for p in range(2)]
        left = jnp.concatenate(
            [place(lefts[p][h].astype(F32), taken) for h in range(2) for p in range(2)], axis=0
        )
        value, taken = rotated(s, 1)
        rights = split(value)
        right = jnp.concatenate([place(rights[h].astype(F32), taken) for h in range(2)], axis=0)
        prod = lax.dot_general(left, right, NT, preferred_element_type=F32)
        tile = (prod[:256, :128] + prod[256:, :128]) + (prod[:256, 128:] + prod[256:, 128:])
        for p in range(2):
            for block in range(N_BL):
                start = p * TILE + block * STRIP
                to = s * 4 + p * 2
                strips[block, to : to + 2] = tile[start : start + STRIP].reshape(2, 8, TILE)
        if s % 4 == 3:
            part = pl.ds(s // 4 * 16, 16 + s // 7)
            for step in range(N_BL):
                other = me[0] ^ step
                copy = pltpu.make_async_copy(
                    strips.at[(other & 3) * 2 + (other >> 2), part],
                    outs[step].at[part],
                    sem_out.at[s // 4 * N_BL + step],
                )
                copy.start()
                leaving.append(copy)
    for copy in leaving:
        copy.wait()


def grid_call(me, counts, tiles, vis, taps, offs):
    hbm = pl.BlockSpec(memory_space=HBM)
    return pl.pallas_call(
        grid_kernel,
        out_shape=[jax.ShapeDtypeStruct((33, 8, TILE), F32)] * N_BL,
        in_specs=[pl.BlockSpec(memory_space=pltpu.SMEM)] + [hbm] * 5,
        out_specs=[hbm] * N_BL,
        scratch_shapes=[
            pltpu.SMEM((1, SLOTS), jnp.int32),
            pltpu.SMEM((1, SLOTS), jnp.int32),
            pltpu.VMEM((SLOTS, 2, CAP), F32),
            pltpu.VMEM((SLOTS, 2, SUP, CAP), F32),
            pltpu.VMEM((SLOTS, 2, CAP), jnp.int32),
            pltpu.VMEM((N_BL, 33, 8, TILE), F32),
            pltpu.SemaphoreType.DMA((4,)),
            pltpu.SemaphoreType.DMA((SLOTS,)),
            pltpu.SemaphoreType.DMA((2 * N_BL,)),
        ],
        compiler_params=pltpu.CompilerParams(vmem_limit_bytes=60 << 20),
        cost_estimate=pl.CostEstimate(flops=4 << 30, bytes_accessed=8 << 20, transcendentals=0),
    )(me, counts, tiles, vis, taps, offs)


def column_kernel(
    side, in_own, in1, in2, in3, in4, in5, in6, in7, taper_own, taper_in, tw, wh, wl, out,
    taper, in0, cells, half, xh, xl, ob, number, place, sem_in,
):
    mine = side[0]
    kept = pl.ds(pl.multiple_of(mine * STRIP, STRIP), STRIP)
    in_a = pltpu.make_async_copy(taper_own.at[kept], taper.at[mine], sem_in.at[0])
    in_b = pltpu.make_async_copy(taper_in, taper.at[1 - mine], sem_in.at[1])
    in_a.start()
    in_b.start()
    in_d = pltpu.make_async_copy(in_own, in0, sem_in.at[3])
    in_d.start()
    strips = [in0, in1, in2, in3, in4, in5, in6, in7]
    for block in range(N_BL):
        rows = slice(block * SLOTS, (block + 1) * SLOTS)
        if block == 0:
            cells[...] = jnp.zeros_like(cells)
            in_d.wait()
        number[rows, :] = strips[block][32].astype(jnp.int32)
    to_scalar = pltpu.make_async_copy(number, place, sem_in.at[2])
    to_scalar.start()
    to_scalar.wait()

    for block in range(N_BL):
        for slot in range(SLOTS):
            tile = place[block * SLOTS + slot, 0]
            cells[tile] = cells[tile] + strips[block][slot * 4 : slot * 4 + 4]
    in_a.wait()
    in_b.wait()
    for tr in range(BANDS):
        for a0 in range(8):
            x = []
            for a1 in range(8):
                a = a1 * 8 + a0
                t = taper[tr, :, a * TILE : (a + 1) * TILE]
                z = cells[tr * COLS + a].reshape(2, STRIP, TILE)
                x.append((z[0] * t, z[1] * t))
            for k0, y in enumerate(dft8(x)):
                if a0 * k0:
                    c, s = unit(64, a0 * k0)
                    y = mul(y, float(c), float(s))
                half[k0 * 8 + a0, 0:16] = y[0]
                half[k0 * 8 + a0, 16:32] = y[1]
        for k0 in range(8):
            x = [(half[k0 * 8 + a0, 0:16], half[k0 * 8 + a0, 16:32]) for a0 in range(8)]
            for k1, y in enumerate(dft8(x)):
                k = k0 + 8 * k1
                y = mul(y, tw[0, k : k + 1, :], tw[1, k : k + 1, :])
                for p in range(2):
                    high, low = split(y[p])
                    xh[tr, k * 16 : k * 16 + 16, p * TILE : (p + 1) * TILE] = high
                    xl[tr, k * 16 : k * 16 + 16, p * TILE : (p + 1) * TILE] = low
        for block in range(4):
            rows_h = xh[tr, block * 256 : (block + 1) * 256, :]
            rows_l = xl[tr, block * 256 : (block + 1) * 256, :]
            prod = lax.dot_general(wh[...], rows_h, NT, preferred_element_type=F32)
            prod += lax.dot_general(wl[...], rows_h, NT, preferred_element_type=F32)
            prod += lax.dot_general(wh[...], rows_l, NT, preferred_element_type=F32)
            kh = block // 2
            for p in range(2):
                for m in range(2):
                    row = tr * 4 + (block % 2) * 2 + m
                    ob[kh, p, row] = prod[p * TILE : (p + 1) * TILE, m * TILE : (m + 1) * TILE]
            if tr == 1 and block % 2 == 1:
                for p in range(2):
                    out[kh, :, p * 8 : p * 8 + 8, :] = jnp.swapaxes(ob[kh, p], 0, 1)


def column_tables():
    k = np.arange(COLS)[:, None]
    y = np.arange(TILE)[None, :]
    turn = np.stack(unit(G, k * y)).astype(np.float32)
    zl, r, yh = np.meshgrid(np.arange(2), np.arange(N_ROW), np.arange(2), indexing="ij")
    q = (r * 4 + zl * 2 + yh).reshape(TILE, 1)
    high, low = halves(real_form(*unit(TILE, q * y)))
    return turn, high, low


def column_call(side, strips, taper_own, taper_in):
    smem = pl.BlockSpec(memory_space=pltpu.SMEM)
    vmem = pl.BlockSpec(memory_space=pltpu.VMEM)
    hbm = pl.BlockSpec(memory_space=pl.ANY)
    return pl.pallas_call(
        column_kernel,
        out_shape=jax.ShapeDtypeStruct((2, TILE, 16, TILE), F32),
        in_specs=[smem, hbm] + [vmem] * (N_BL - 1) + [hbm, hbm, vmem, vmem, vmem],
        out_specs=vmem,
        scratch_shapes=[
            pltpu.VMEM((2, STRIP, G), F32),
            pltpu.VMEM((33, 8, TILE), F32),
            pltpu.VMEM((BANDS * COLS, 4, 8, TILE), F32),
            pltpu.VMEM((64, 32, TILE), F32),
            pltpu.VMEM((BANDS, 1024, 256), BF16),
            pltpu.VMEM((BANDS, 1024, 256), BF16),
            pltpu.VMEM((2, 2, 8, TILE, TILE), F32),
            pltpu.VMEM((64, TILE), jnp.int32),
            pltpu.SMEM((64, TILE), jnp.int32),
            pltpu.SemaphoreType.DMA((4,)),
        ],
        compiler_params=pltpu.CompilerParams(vmem_limit_bytes=40 << 20),
    )(side, *strips, taper_own, taper_in, *column_tables())


def row_kernel(arrived, w1h, w1l, tw, gh, gl, out, xh, xl, at, bh, bl):
    for dl in range(4):
        for half in range(2):
            rows = jnp.swapaxes(arrived[dl, :, half * 8 : half * 8 + 8, :], 0, 1)
            for t in range(8):
                to = (half * 2 + t // 4) * 64
                lanes = (t % 4) * TILE
                high, low = split(rows[t])
                xh[dl, to : to + 64, lanes : lanes + TILE] = high
                xl[dl, to : to + 64, lanes : lanes + TILE] = low
        prod = jnp.dot(w1h[...], xh[dl], preferred_element_type=F32)
        prod += jnp.dot(w1l[...], xh[dl], preferred_element_type=F32)
        prod += jnp.dot(w1h[...], xl[dl], preferred_element_type=F32)
        at[dl] = prod

    def radix(step, carry):
        mb, block = step // 8, step % 8
        rows = pl.ds(pl.multiple_of(block * 16, 16), 16)
        rows_im = pl.ds(pl.multiple_of(TILE + block * 16, 16), 16)
        lanes = pl.ds(pl.multiple_of(mb * TILE, TILE), TILE)
        parts = [
            mul((at[dl, rows, lanes], at[dl, rows_im, lanes]), tw[dl, 0, rows, :], tw[dl, 1, rows, :])
            for dl in range(4)
        ]
        to_rows = pl.ds(pl.multiple_of(mb * TILE + block * 16, 16), 16)
        for kb, y in enumerate(dft4(*parts)):
            for p in range(2):
                high, low = split(y[p])
                bh[kb, to_rows, p * TILE : (p + 1) * TILE] = high
                bl[kb, to_rows, p * TILE : (p + 1) * TILE] = low
        return carry

    lax.fori_loop(0, 32, radix, 0)
    for kb in range(4):
        prod = lax.dot_general(gh[kb], bh[kb], NT, preferred_element_type=F32)
        prod += lax.dot_general(gl[kb], bh[kb], NT, preferred_element_type=F32)
        prod += lax.dot_general(gh[kb], bl[kb], NT, preferred_element_type=F32)
        for p in range(2):
            for k2 in range(16):
                row = p * TILE + k2 * 8
                to = (k2 * 4 + kb) * TILE
                for mb in range(4):
                    out[p, mb * 8 : mb * 8 + 8, to : to + TILE] = prod[
                        row : row + 8, mb * TILE : (mb + 1) * TILE
                    ]


def row_tables():
    ka = np.arange(TILE)[:, None]
    tr, r, yh = np.meshgrid(np.arange(2), np.arange(N_ROW), np.arange(2), indexing="ij")
    coarse = (r * 4 + tr * 2 + yh).reshape(1, TILE)
    w1h, w1l = halves(real_form(*unit(TILE, ka * coarse)))
    fine = np.arange(TILE)[None, :] % 16
    turn = np.stack([np.stack(unit(G, ka * (dl * 16 + fine))) for dl in range(4)])
    k2, j = np.meshgrid(np.arange(16), np.arange(8), indexing="ij")
    k2, j = k2.reshape(TILE, 1), j.reshape(TILE, 1)
    jj, i = np.meshgrid(np.arange(8), np.arange(16), indexing="ij")
    jj, i = jj.reshape(1, TILE), i.reshape(1, TILE)
    same = (j == jj) / G
    last = []
    for kb in range(4):
        cosine, sine = unit(64, i * (kb + 4 * k2))
        last.append(real_form(cosine * same, sine * same))
    gh, gl = halves(np.stack(last))
    return w1h, w1l, turn.astype(np.float32), gh, gl


def row_call(arrived):
    vmem = pl.BlockSpec(memory_space=pltpu.VMEM)
    return pl.pallas_call(
        row_kernel,
        out_shape=jax.ShapeDtypeStruct((2, 32, G), F32),
        in_specs=[vmem, vmem, vmem, vmem, vmem, vmem],
        out_specs=vmem,
        scratch_shapes=[
            pltpu.VMEM((4, 256, 512), BF16),
            pltpu.VMEM((4, 256, 512), BF16),
            pltpu.VMEM((4, 256, 512), F32),
            pltpu.VMEM((4, 512, 256), BF16),
            pltpu.VMEM((4, 512, 256), BF16),
        ],
        compiler_params=pltpu.CompilerParams(vmem_limit_bytes=40 << 20),
    )(arrived, *row_tables())


def body(visibilities, kernels, offsets, counts, slot_tiles, taper):
    me = lax.axis_index("bl")
    side = me // 4
    swap = [(s, s ^ 4) for s in range(N_BL)]
    given = lax.dynamic_slice(taper, ((1 - side) * STRIP, 0), (STRIP, G))
    taper_in = lax.ppermute(given, "bl", swap)
    strips = grid_call(
        me.reshape(1).astype(jnp.int32), counts[0], slot_tiles[0], visibilities[0, 0], kernels[0, 0], offsets[0, 0]
    )
    far, taper_in = lax.optimization_barrier((list(strips[4:]), taper_in))
    blocks = list(strips[:4]) + far
    strips = [blocks[0]] + [
        lax.ppermute(blocks[step], "bl", [(s, s ^ step) for s in range(N_BL)])
        for step in range(1, N_BL)
    ]
    side = side.reshape(1).astype(jnp.int32)
    leaving = column_call(side, strips, taper, taper_in)
    arrived = lax.all_to_all(
        leaving.reshape(256, 16, TILE), ("bl", "row"), 0, 0, axis_index_groups=members(), tiled=True
    )
    return row_call(arrived.reshape(4, 64, 16, TILE))


def members():
    group = []
    for yl in range(2):
        for zl in range(2):
            for r in range(N_ROW):
                for yh in range(2):
                    group.append((zl * 4 + yh * 2 + yl) * N_ROW + r)
    return [group]


def solution(mesh):
    in_specs = (
        P("bl", "row", None, None, None),
        P("bl", "row", None, None, None, None),
        P("bl", "row", None, None, None),
        P("bl", "row", None),
        P("bl", "row", None),
        P(("row", "bl"), None),
    )
    out_specs = P(None, ("row", "bl"), None)
    return jax.shard_map(body, mesh=mesh, in_specs=in_specs, out_specs=out_specs, check_vma=False)
```

```python
import math

import jax
import jax.numpy as jnp
import ml_dtypes
import numpy as np
from jax import lax
from jax.experimental import pallas as pl
from jax.experimental.pallas import tpu as pltpu
from jax.sharding import PartitionSpec as P

G = 8192
TILE = 128
SUP = 8
SLOTS = 8
CAP = 768
N_BL = 8
N_ROW = 32
BANDS = 2
STRIP = TILE // N_BL
COLS = G // TILE
F32 = jnp.float32
BF16 = jnp.bfloat16
HBM = pltpu.MemorySpace.HBM
NT = (((1,), (1,)), ((), ()))


def unit(length, phase):
    angle = 2.0 * np.pi * (np.asarray(phase, np.int64) % length) / length
    return np.cos(angle), np.sin(angle)


def real_form(cosine, sine):
    return np.block([[cosine, sine], [-sine, cosine]])


def halves(table):
    high = table.astype(ml_dtypes.bfloat16)
    low = (table - high.astype(np.float64)).astype(ml_dtypes.bfloat16)
    return high, low


def split(value):
    high = value.astype(BF16)
    low = (value - high.astype(F32)).astype(BF16)
    return high, low


def add(left, right):
    return (left[0] + right[0], left[1] + right[1])


def sub(left, right):
    return (left[0] - right[0], left[1] - right[1])


def dft4(a, b, c, d):
    s, t = add(a, c), sub(a, c)
    u, v = add(b, d), sub(b, d)
    w = (v[1], -v[0])
    return [add(s, u), add(t, w), sub(s, u), sub(t, w)]


def dft8(x):
    even = dft4(x[0], x[2], x[4], x[6])
    odd = dft4(x[1], x[3], x[5], x[7])
    r = math.sqrt(0.5)
    turned = [
        odd[0],
        ((odd[1][0] + odd[1][1]) * r, (odd[1][1] - odd[1][0]) * r),
        (odd[2][1], -odd[2][0]),
        ((odd[3][1] - odd[3][0]) * r, (odd[3][1] + odd[3][0]) * -r),
    ]
    return [add(e, o) for e, o in zip(even, turned)] + [sub(e, o) for e, o in zip(even, turned)]


def mul(x, cosine, sine):
    return (x[0] * cosine + x[1] * sine, x[1] * cosine - x[0] * sine)


def grid_kernel(
    me, counts_in, tiles_in, vis_in, taps_in, offs_in,
    out0, out1, out2, out3, out4, out5, out6, out7,
    counts, tiles, vis, taps, offs, strips, sem_few, sem_in, sem_out,
):
    outs = [out0, out1, out2, out3, out4, out5, out6, out7]
    few = [
        pltpu.make_async_copy(counts_in, counts, sem_few.at[0]),
        pltpu.make_async_copy(tiles_in, tiles, sem_few.at[1]),
        pltpu.make_async_copy(vis_in, vis, sem_few.at[2]),
        pltpu.make_async_copy(offs_in, offs, sem_few.at[3]),
    ]
    for copy in few:
        copy.start()
    tap_copies = []
    for s in range(SLOTS):
        copy = pltpu.make_async_copy(taps_in.at[s], taps.at[s], sem_in.at[s])
        copy.start()
        tap_copies.append(copy)
    for copy in few:
        copy.wait()
    sub_index = lax.broadcasted_iota(jnp.int32, (SUP, CAP), 0)
    lane = lax.broadcasted_iota(jnp.int32, (1, CAP), 1)
    slot_index = lax.broadcasted_iota(jnp.int32, (SLOTS, TILE), 0)
    numbers = jnp.zeros((SLOTS, TILE), jnp.int32)
    for s in range(SLOTS):
        numbers = jnp.where(slot_index == s, tiles[0, s], numbers)
    for block in range(N_BL):
        strips[block, 32] = numbers.astype(F32)
    leaving = []

    def place(block, taken):
        pieces = [jnp.where(taken == x, block, 0.0) for x in range(TILE // SUP)]
        return jnp.concatenate(pieces, axis=0).astype(BF16)

    def rotated(s, axis):
        first = jnp.broadcast_to(offs[s, axis : axis + 1, :], (SUP, CAP))
        shift = first & (SUP - 1)
        value = taps[s, axis]
        for bit in (1, 2, 4):
            value = jnp.where((shift & bit) != 0, pltpu.roll(value, bit, 0), value)
        taken = (first >> 3) + jnp.where(sub_index < shift, 1, 0)
        return value, taken

    for s in range(SLOTS):
        tap_copies[s].wait()
        live = lane < counts[0, s]
        value, taken = rotated(s, 0)
        lefts = [split(value * jnp.where(live, vis[s, p : p + 1, :], 0.0)) for p in range(2)]
        left = jnp.concatenate(
            [place(lefts[p][h].astype(F32), taken) for h in range(2) for p in range(2)], axis=0
        )
        value, taken = rotated(s, 1)
        rights = split(value)
        right = jnp.concatenate([place(rights[h].astype(F32), taken) for h in range(2)], axis=0)
        prod = lax.dot_general(left[:256], right, NT, preferred_element_type=F32)
        tile = prod[:, :128] + prod[:, 128:]
        tile += lax.dot_general(left[256:], right[:128], NT, preferred_element_type=F32)
        for p in range(2):
            for block in range(N_BL):
                start = p * TILE + block * STRIP
                to = s * 4 + p * 2
                strips[block, to : to + 2] = tile[start : start + STRIP].reshape(2, 8, TILE)
        if s % 4 == 3:
            part = pl.ds(s // 4 * 16, 16 + s // 7)
            for step in range(N_BL):
                other = me[0] ^ step
                copy = pltpu.make_async_copy(
                    strips.at[(other & 3) * 2 + (other >> 2), part],
                    outs[step].at[part],
                    sem_out.at[s // 4 * N_BL + step],
                )
                copy.start()
                leaving.append(copy)
    for copy in leaving:
        copy.wait()


def grid_call(me, counts, tiles, vis, taps, offs):
    hbm = pl.BlockSpec(memory_space=HBM)
    return pl.pallas_call(
        grid_kernel,
        out_shape=[jax.ShapeDtypeStruct((33, 8, TILE), F32)] * N_BL,
        in_specs=[pl.BlockSpec(memory_space=pltpu.SMEM)] + [hbm] * 5,
        out_specs=[pl.BlockSpec(memory_space=pltpu.VMEM)] + [hbm] * (N_BL - 1),
        scratch_shapes=[
            pltpu.SMEM((1, SLOTS), jnp.int32),
            pltpu.SMEM((1, SLOTS), jnp.int32),
            pltpu.VMEM((SLOTS, 2, CAP), F32),
            pltpu.VMEM((SLOTS, 2, SUP, CAP), F32),
            pltpu.VMEM((SLOTS, 2, CAP), jnp.int32),
            pltpu.VMEM((N_BL, 33, 8, TILE), F32),
            pltpu.SemaphoreType.DMA((4,)),
            pltpu.SemaphoreType.DMA((SLOTS,)),
            pltpu.SemaphoreType.DMA((2 * N_BL,)),
        ],
        compiler_params=pltpu.CompilerParams(vmem_limit_bytes=60 << 20),
        cost_estimate=pl.CostEstimate(flops=4 << 30, bytes_accessed=8 << 20, transcendentals=0),
    )(me, counts, tiles, vis, taps, offs)


def column_kernel(
    side, in0, in1, in2, in3, in4, in5, in6, in7, taper_own, taper_in, tw, wh, wl, out,
    taper, cells, half, xh, xl, ob, number, place, sem_in,
):
    mine = side[0]
    kept = pl.ds(pl.multiple_of(mine * STRIP, STRIP), STRIP)
    in_a = pltpu.make_async_copy(taper_own.at[kept], taper.at[mine], sem_in.at[0])
    in_b = pltpu.make_async_copy(taper_in, taper.at[1 - mine], sem_in.at[1])
    in_a.start()
    in_b.start()
    strips = [in0, in1, in2, in3, in4, in5, in6, in7]
    for block in range(N_BL):
        rows = slice(block * SLOTS, (block + 1) * SLOTS)
        number[rows, :] = strips[block][32].astype(jnp.int32)
    to_scalar = pltpu.make_async_copy(number, place, sem_in.at[2])
    to_scalar.start()
    cells[...] = jnp.zeros_like(cells)
    to_scalar.wait()

    for block in range(N_BL):
        tiles = [place[block * SLOTS + slot, 0] for slot in range(SLOTS)]
        sums = [
            cells[tile] + strips[block][slot * 4 : slot * 4 + 4] for slot, tile in enumerate(tiles)
        ]
        for tile, value in zip(tiles, sums):
            cells[tile] = value
    in_a.wait()
    in_b.wait()
    for tr in range(BANDS):
        for a0 in range(8):
            x = []
            for a1 in range(8):
                a = a1 * 8 + a0
                t = taper[tr, :, a * TILE : (a + 1) * TILE]
                z = cells[tr * COLS + a].reshape(2, STRIP, TILE)
                x.append((z[0] * t, z[1] * t))
            for k0, y in enumerate(dft8(x)):
                if a0 * k0:
                    c, s = unit(64, a0 * k0)
                    y = mul(y, float(c), float(s))
                half[k0 * 8 + a0, 0:16] = y[0]
                half[k0 * 8 + a0, 16:32] = y[1]
        for k0 in range(8):
            x = [(half[k0 * 8 + a0, 0:16], half[k0 * 8 + a0, 16:32]) for a0 in range(8)]
            for k1, y in enumerate(dft8(x)):
                k = k0 + 8 * k1
                y = mul(y, tw[0, k : k + 1, :], tw[1, k : k + 1, :])
                for p in range(2):
                    high, low = split(y[p])
                    xh[tr, k * 16 : k * 16 + 16, p * TILE : (p + 1) * TILE] = high
                    xl[tr, k * 16 : k * 16 + 16, p * TILE : (p + 1) * TILE] = low
        for block in range(4):
            rows_h = xh[tr, block * 256 : (block + 1) * 256, :]
            rows_l = xl[tr, block * 256 : (block + 1) * 256, :]
            prod = lax.dot_general(wh[...], rows_h, NT, preferred_element_type=F32)
            prod += lax.dot_general(wl[...], rows_h, NT, preferred_element_type=F32)
            prod += lax.dot_general(wh[...], rows_l, NT, preferred_element_type=F32)
            kh = block // 2
            for p in range(2):
                for m in range(2):
                    row = tr * 4 + (block % 2) * 2 + m
                    ob[kh, p, row] = prod[p * TILE : (p + 1) * TILE, m * TILE : (m + 1) * TILE]
            if tr == 1 and block % 2 == 1:
                for p in range(2):
                    out[kh, :, p * 8 : p * 8 + 8, :] = jnp.swapaxes(ob[kh, p], 0, 1)


def column_tables():
    k = np.arange(COLS)[:, None]
    y = np.arange(TILE)[None, :]
    turn = np.stack(unit(G, k * y)).astype(np.float32)
    zl, r, yh = np.meshgrid(np.arange(2), np.arange(N_ROW), np.arange(2), indexing="ij")
    q = (r * 4 + zl * 2 + yh).reshape(TILE, 1)
    high, low = halves(real_form(*unit(TILE, q * y)))
    return turn, high, low


def column_call(side, strips, taper_own, taper_in):
    smem = pl.BlockSpec(memory_space=pltpu.SMEM)
    vmem = pl.BlockSpec(memory_space=pltpu.VMEM)
    hbm = pl.BlockSpec(memory_space=pl.ANY)
    return pl.pallas_call(
        column_kernel,
        out_shape=jax.ShapeDtypeStruct((2, TILE, 16, TILE), F32),
        in_specs=[smem] + [vmem] * N_BL + [hbm, hbm, vmem, vmem, vmem],
        out_specs=vmem,
        scratch_shapes=[
            pltpu.VMEM((2, STRIP, G), F32),
            pltpu.VMEM((BANDS * COLS, 4, 8, TILE), F32),
            pltpu.VMEM((64, 32, TILE), F32),
            pltpu.VMEM((BANDS, 1024, 256), BF16),
            pltpu.VMEM((BANDS, 1024, 256), BF16),
            pltpu.VMEM((2, 2, 8, TILE, TILE), F32),
            pltpu.VMEM((64, TILE), jnp.int32),
            pltpu.SMEM((64, TILE), jnp.int32),
            pltpu.SemaphoreType.DMA((3,)),
        ],
        compiler_params=pltpu.CompilerParams(vmem_limit_bytes=40 << 20),
    )(side, *strips, taper_own, taper_in, *column_tables())


def row_kernel(arrived, w1h, w1l, tw, gh, gl, out, xh, xl, at, bh, bl, image, sem):
    for dl in range(4):
        for half in range(2):
            rows = jnp.swapaxes(arrived[dl, :, half * 8 : half * 8 + 8, :], 0, 1)
            for t in range(8):
                to = (half * 2 + t // 4) * 64
                lanes = (t % 4) * TILE
                high, low = split(rows[t])
                xh[dl, to : to + 64, lanes : lanes + TILE] = high
                xl[dl, to : to + 64, lanes : lanes + TILE] = low
        prod = jnp.dot(w1h[...], xh[dl], preferred_element_type=F32)
        prod += jnp.dot(w1l[...], xh[dl], preferred_element_type=F32)
        prod += jnp.dot(w1h[...], xl[dl], preferred_element_type=F32)
        at[dl] = prod

    def radix(step, carry):
        mb, block = step // 8, step % 8
        rows = pl.ds(pl.multiple_of(block * 16, 16), 16)
        rows_im = pl.ds(pl.multiple_of(TILE + block * 16, 16), 16)
        lanes = pl.ds(pl.multiple_of(mb * TILE, TILE), TILE)
        parts = [
            mul((at[dl, rows, lanes], at[dl, rows_im, lanes]), tw[dl, 0, rows, :], tw[dl, 1, rows, :])
            for dl in range(4)
        ]
        to_rows = pl.ds(pl.multiple_of(mb * TILE + block * 16, 16), 16)
        for kb, y in enumerate(dft4(*parts)):
            for p in range(2):
                high, low = split(y[p])
                bh[kb, to_rows, p * TILE : (p + 1) * TILE] = high
                bl[kb, to_rows, p * TILE : (p + 1) * TILE] = low
        return carry

    lax.fori_loop(0, 32, radix, 0, unroll=4)
    copies = []
    for half in range(2):
        rows = slice(half * 256, half * 256 + 256)
        for kb in range(4):
            prod = lax.dot_general(gh[kb], bh[kb, rows], NT, preferred_element_type=F32)
            prod += lax.dot_general(gl[kb], bh[kb, rows], NT, preferred_element_type=F32)
            prod += lax.dot_general(gh[kb], bl[kb, rows], NT, preferred_element_type=F32)
            for p in range(2):
                for k2 in range(16):
                    row = p * TILE + k2 * 8
                    to = (k2 * 4 + kb) * TILE
                    for m in range(2):
                        image[half, p, m * 8 : m * 8 + 8, to : to + TILE] = prod[
                            row : row + 8, m * TILE : (m + 1) * TILE
                        ]
        copy = pltpu.make_async_copy(
            image.at[half], out.at[:, pl.ds(half * 16, 16), :], sem.at[half]
        )
        copy.start()
        copies.append(copy)
    for copy in copies:
        copy.wait()


def row_tables():
    ka = np.arange(TILE)[:, None]
    tr, r, yh = np.meshgrid(np.arange(2), np.arange(N_ROW), np.arange(2), indexing="ij")
    coarse = (r * 4 + tr * 2 + yh).reshape(1, TILE)
    w1h, w1l = halves(real_form(*unit(TILE, ka * coarse)))
    fine = np.arange(TILE)[None, :] % 16
    turn = np.stack([np.stack(unit(G, ka * (dl * 16 + fine))) for dl in range(4)])
    k2, j = np.meshgrid(np.arange(16), np.arange(8), indexing="ij")
    k2, j = k2.reshape(TILE, 1), j.reshape(TILE, 1)
    jj, i = np.meshgrid(np.arange(8), np.arange(16), indexing="ij")
    jj, i = jj.reshape(1, TILE), i.reshape(1, TILE)
    same = (j == jj) / G
    last = []
    for kb in range(4):
        cosine, sine = unit(64, i * (kb + 4 * k2))
        last.append(real_form(cosine * same, sine * same))
    gh, gl = halves(np.stack(last))
    return w1h, w1l, turn.astype(np.float32), gh, gl


def row_call(arrived):
    vmem = pl.BlockSpec(memory_space=pltpu.VMEM)
    return pl.pallas_call(
        row_kernel,
        out_shape=jax.ShapeDtypeStruct((2, 32, G), F32),
        in_specs=[vmem, vmem, vmem, vmem, vmem, vmem],
        out_specs=pl.BlockSpec(memory_space=HBM),
        scratch_shapes=[
            pltpu.VMEM((4, 256, 512), BF16),
            pltpu.VMEM((4, 256, 512), BF16),
            pltpu.VMEM((4, 256, 512), F32),
            pltpu.VMEM((4, 512, 256), BF16),
            pltpu.VMEM((4, 512, 256), BF16),
            pltpu.VMEM((2, 2, 16, G), F32),
            pltpu.SemaphoreType.DMA((2,)),
        ],
        compiler_params=pltpu.CompilerParams(vmem_limit_bytes=40 << 20),
    )(arrived, *row_tables())


def body(visibilities, kernels, offsets, counts, slot_tiles, taper):
    me = lax.axis_index("bl")
    side = me // 4
    swap = [(s, s ^ 4) for s in range(N_BL)]
    given = lax.dynamic_slice(taper, ((1 - side) * STRIP, 0), (STRIP, G))
    taper_in = lax.ppermute(given, "bl", swap)
    strips = grid_call(
        me.reshape(1).astype(jnp.int32), counts[0], slot_tiles[0], visibilities[0, 0], kernels[0, 0], offsets[0, 0]
    )
    far, taper_in = lax.optimization_barrier((list(strips[5:]), taper_in))
    blocks = list(strips[:5]) + far
    strips = [blocks[0]] + [
        lax.ppermute(blocks[step], "bl", [(s, s ^ step) for s in range(N_BL)])
        for step in range(1, N_BL)
    ]
    side = side.reshape(1).astype(jnp.int32)
    leaving = column_call(side, strips, taper, taper_in)
    arrived = lax.all_to_all(
        leaving.reshape(256, 16, TILE), ("bl", "row"), 0, 0, axis_index_groups=members(), tiled=True
    )
    return row_call(arrived.reshape(4, 64, 16, TILE))


def members():
    group = []
    for yl in range(2):
        for zl in range(2):
            for r in range(N_ROW):
                for yh in range(2):
                    group.append((zl * 4 + yh * 2 + yl) * N_ROW + r)
    return [group]


def solution(mesh):
    in_specs = (
        P("bl", "row", None, None, None),
        P("bl", "row", None, None, None, None),
        P("bl", "row", None, None, None),
        P("bl", "row", None),
        P("bl", "row", None),
        P(("row", "bl"), None),
    )
    out_specs = P(None, ("row", "bl"), None)
    return jax.shard_map(body, mesh=mesh, in_specs=in_specs, out_specs=out_specs, check_vma=False)
```

```python
import math

import jax
import jax.numpy as jnp
import ml_dtypes
import numpy as np
from jax import lax
from jax.experimental import pallas as pl
from jax.experimental.pallas import tpu as pltpu
from jax.sharding import PartitionSpec as P

G = 8192
TILE = 128
SUP = 8
SLOTS = 8
CAP = 768
N_BL = 8
N_ROW = 32
BANDS = 2
STRIP = TILE // N_BL
STEPS = (0, 1, 2, 3, 4, 5, 6, 7)
FREE = 6
COLS = G // TILE
F32 = jnp.float32
BF16 = jnp.bfloat16
HBM = pltpu.MemorySpace.HBM
NT = (((1,), (1,)), ((), ()))


def unit(length, phase):
    angle = 2.0 * np.pi * (np.asarray(phase, np.int64) % length) / length
    return np.cos(angle), np.sin(angle)


def real_form(cosine, sine):
    return np.block([[cosine, sine], [-sine, cosine]])


def halves(table):
    high = table.astype(ml_dtypes.bfloat16)
    low = (table - high.astype(np.float64)).astype(ml_dtypes.bfloat16)
    return high, low


def split(value):
    high = value.astype(BF16)
    low = (value - high.astype(F32)).astype(BF16)
    return high, low


def add(left, right):
    return (left[0] + right[0], left[1] + right[1])


def sub(left, right):
    return (left[0] - right[0], left[1] - right[1])


def dft4(a, b, c, d):
    s, t = add(a, c), sub(a, c)
    u, v = add(b, d), sub(b, d)
    w = (v[1], -v[0])
    return [add(s, u), add(t, w), sub(s, u), sub(t, w)]


def dft8(x):
    even = dft4(x[0], x[2], x[4], x[6])
    odd = dft4(x[1], x[3], x[5], x[7])
    r = math.sqrt(0.5)
    turned = [
        odd[0],
        ((odd[1][0] + odd[1][1]) * r, (odd[1][1] - odd[1][0]) * r),
        (odd[2][1], -odd[2][0]),
        ((odd[3][1] - odd[3][0]) * r, (odd[3][1] + odd[3][0]) * -r),
    ]
    return [add(e, o) for e, o in zip(even, turned)] + [sub(e, o) for e, o in zip(even, turned)]


def mul(x, cosine, sine):
    return (x[0] * cosine + x[1] * sine, x[1] * cosine - x[0] * sine)


def grid_kernel(
    me, counts_in, tiles_in, vis_in, taps_in, offs_in,
    out0, out1, out2, out3, out4, out5, out6, out7,
    counts, tiles, vis, taps, offs, strips, sem_few, sem_in, sem_out,
):
    outs = [out0, out1, out2, out3, out4, out5, out6, out7]
    few = [
        pltpu.make_async_copy(counts_in, counts, sem_few.at[0]),
        pltpu.make_async_copy(tiles_in, tiles, sem_few.at[1]),
        pltpu.make_async_copy(vis_in, vis, sem_few.at[2]),
        pltpu.make_async_copy(offs_in, offs, sem_few.at[3]),
    ]
    for copy in few:
        copy.start()
    tap_copies = []
    for s in range(SLOTS):
        copy = pltpu.make_async_copy(taps_in.at[s], taps.at[s], sem_in.at[s])
        copy.start()
        tap_copies.append(copy)
    for copy in few:
        copy.wait()
    sub_index = lax.broadcasted_iota(jnp.int32, (SUP, CAP), 0)
    lane = lax.broadcasted_iota(jnp.int32, (1, CAP), 1)
    slot_index = lax.broadcasted_iota(jnp.int32, (SLOTS, TILE), 0)
    numbers = jnp.zeros((SLOTS, TILE), jnp.int32)
    for s in range(SLOTS):
        numbers = jnp.where(slot_index == s, tiles[0, s], numbers)
    for block in range(N_BL):
        strips[block, 32] = numbers.astype(F32)
    leaving = []

    def place(block, taken):
        pieces = [jnp.where(taken == x, block, 0.0) for x in range(TILE // SUP)]
        return jnp.concatenate(pieces, axis=0).astype(BF16)

    def rotated(s, axis):
        first = jnp.broadcast_to(offs[s, axis : axis + 1, :], (SUP, CAP))
        shift = first & (SUP - 1)
        value = taps[s, axis]
        for bit in (1, 2, 4):
            value = jnp.where((shift & bit) != 0, pltpu.roll(value, bit, 0), value)
        taken = (first >> 3) + jnp.where(sub_index < shift, 1, 0)
        return value, taken

    for s in range(SLOTS):
        tap_copies[s].wait()
        live = lane < counts[0, s]
        value, taken = rotated(s, 0)
        lefts = [split(value * jnp.where(live, vis[s, p : p + 1, :], 0.0)) for p in range(2)]
        left = jnp.concatenate(
            [place(lefts[p][h].astype(F32), taken) for h in range(2) for p in range(2)], axis=0
        )
        value, taken = rotated(s, 1)
        rights = split(value)
        right = jnp.concatenate([place(rights[h].astype(F32), taken) for h in range(2)], axis=0)
        prod = lax.dot_general(left[:256], right, NT, preferred_element_type=F32)
        tile = prod[:, :128] + prod[:, 128:]
        tile += lax.dot_general(left[256:], right[:128], NT, preferred_element_type=F32)
        for p in range(2):
            for block in range(N_BL):
                start = p * TILE + block * STRIP
                to = s * 4 + p * 2
                strips[block, to : to + 2] = tile[start : start + STRIP].reshape(2, 8, TILE)
        if s % 4 == 3:
            part = pl.ds(s // 4 * 16, 16 + s // 7)
            for step in range(N_BL):
                other = me[0] ^ STEPS[step]
                copy = pltpu.make_async_copy(
                    strips.at[(other & 3) * 2 + (other >> 2), part],
                    outs[step].at[part],
                    sem_out.at[s // 4 * N_BL + step],
                )
                copy.start()
                leaving.append(copy)
    for copy in leaving:
        copy.wait()


def grid_call(me, counts, tiles, vis, taps, offs):
    hbm = pl.BlockSpec(memory_space=HBM)
    return pl.pallas_call(
        grid_kernel,
        out_shape=[jax.ShapeDtypeStruct((33, 8, TILE), F32)] * N_BL,
        in_specs=[pl.BlockSpec(memory_space=pltpu.SMEM)] + [hbm] * 5,
        out_specs=[pl.BlockSpec(memory_space=pltpu.VMEM)] + [hbm] * (N_BL - 1),
        scratch_shapes=[
            pltpu.SMEM((1, SLOTS), jnp.int32),
            pltpu.SMEM((1, SLOTS), jnp.int32),
            pltpu.VMEM((SLOTS, 2, CAP), F32),
            pltpu.VMEM((SLOTS, 2, SUP, CAP), F32),
            pltpu.VMEM((SLOTS, 2, CAP), jnp.int32),
            pltpu.VMEM((N_BL, 33, 8, TILE), F32),
            pltpu.SemaphoreType.DMA((4,)),
            pltpu.SemaphoreType.DMA((SLOTS,)),
            pltpu.SemaphoreType.DMA((2 * N_BL,)),
        ],
        compiler_params=pltpu.CompilerParams(vmem_limit_bytes=60 << 20),
        cost_estimate=pl.CostEstimate(flops=4 << 30, bytes_accessed=8 << 20, transcendentals=0),
    )(me, counts, tiles, vis, taps, offs)


def column_kernel(
    side, in0, in1, in2, in3, in4, in5, in6, in7, taper_own, taper_in, tw, wh, wl, out,
    taper, cells, half, xh, xl, ob, number, place, sem_in,
):
    mine = side[0]
    kept = pl.ds(pl.multiple_of(mine * STRIP, STRIP), STRIP)
    in_a = pltpu.make_async_copy(taper_own.at[kept], taper.at[mine], sem_in.at[0])
    in_b = pltpu.make_async_copy(taper_in, taper.at[1 - mine], sem_in.at[1])
    in_a.start()
    in_b.start()
    strips = [in0, in1, in2, in3, in4, in5, in6, in7]
    for block in range(N_BL):
        rows = slice(block * SLOTS, (block + 1) * SLOTS)
        number[rows, :] = strips[block][32].astype(jnp.int32)
    to_scalar = pltpu.make_async_copy(number, place, sem_in.at[2])
    to_scalar.start()
    cells[...] = jnp.zeros_like(cells)
    to_scalar.wait()

    for block in range(N_BL):
        tiles = [place[block * SLOTS + slot, 0] for slot in range(SLOTS)]
        sums = [
            cells[tile] + strips[block][slot * 4 : slot * 4 + 4] for slot, tile in enumerate(tiles)
        ]
        for tile, value in zip(tiles, sums):
            cells[tile] = value
    in_a.wait()
    in_b.wait()
    for tr in range(BANDS):
        for a0 in range(8):
            x = []
            for a1 in range(8):
                a = a1 * 8 + a0
                t = taper[tr, :, a * TILE : (a + 1) * TILE]
                z = cells[tr * COLS + a].reshape(2, STRIP, TILE)
                x.append((z[0] * t, z[1] * t))
            for k0, y in enumerate(dft8(x)):
                if a0 * k0:
                    c, s = unit(64, a0 * k0)
                    y = mul(y, float(c), float(s))
                half[k0 * 8 + a0, 0:16] = y[0]
                half[k0 * 8 + a0, 16:32] = y[1]
        for k0 in range(8):
            x = [(half[k0 * 8 + a0, 0:16], half[k0 * 8 + a0, 16:32]) for a0 in range(8)]
            for k1, y in enumerate(dft8(x)):
                k = k0 + 8 * k1
                y = mul(y, tw[0, k : k + 1, :], tw[1, k : k + 1, :])
                for p in range(2):
                    high, low = split(y[p])
                    xh[tr, k * 16 : k * 16 + 16, p * TILE : (p + 1) * TILE] = high
                    xl[tr, k * 16 : k * 16 + 16, p * TILE : (p + 1) * TILE] = low
        for block in range(4):
            rows_h = xh[tr, block * 256 : (block + 1) * 256, :]
            rows_l = xl[tr, block * 256 : (block + 1) * 256, :]
            prod = lax.dot_general(wh[...], rows_h, NT, preferred_element_type=F32)
            prod += lax.dot_general(wl[...], rows_h, NT, preferred_element_type=F32)
            prod += lax.dot_general(wh[...], rows_l, NT, preferred_element_type=F32)
            kh = block // 2
            for p in range(2):
                for m in range(2):
                    row = tr * 4 + (block % 2) * 2 + m
                    ob[kh, p, row] = prod[p * TILE : (p + 1) * TILE, m * TILE : (m + 1) * TILE]
            if tr == 1 and block % 2 == 1:
                for p in range(2):
                    out[kh, :, p * 8 : p * 8 + 8, :] = jnp.swapaxes(ob[kh, p], 0, 1)


def column_tables():
    k = np.arange(COLS)[:, None]
    y = np.arange(TILE)[None, :]
    turn = np.stack(unit(G, k * y)).astype(np.float32)
    zl, r, yh = np.meshgrid(np.arange(2), np.arange(N_ROW), np.arange(2), indexing="ij")
    q = (r * 4 + zl * 2 + yh).reshape(TILE, 1)
    high, low = halves(real_form(*unit(TILE, q * y)))
    return turn, high, low


def column_call(side, strips, taper_own, taper_in):
    smem = pl.BlockSpec(memory_space=pltpu.SMEM)
    vmem = pl.BlockSpec(memory_space=pltpu.VMEM)
    hbm = pl.BlockSpec(memory_space=pl.ANY)
    return pl.pallas_call(
        column_kernel,
        out_shape=jax.ShapeDtypeStruct((2, TILE, 16, TILE), F32),
        in_specs=[smem] + [vmem] * N_BL + [hbm, hbm, vmem, vmem, vmem],
        out_specs=vmem,
        scratch_shapes=[
            pltpu.VMEM((2, STRIP, G), F32),
            pltpu.VMEM((BANDS * COLS, 4, 8, TILE), F32),
            pltpu.VMEM((64, 32, TILE), F32),
            pltpu.VMEM((BANDS, 1024, 256), BF16),
            pltpu.VMEM((BANDS, 1024, 256), BF16),
            pltpu.VMEM((2, 2, 8, TILE, TILE), F32),
            pltpu.VMEM((64, TILE), jnp.int32),
            pltpu.SMEM((64, TILE), jnp.int32),
            pltpu.SemaphoreType.DMA((3,)),
        ],
        compiler_params=pltpu.CompilerParams(vmem_limit_bytes=40 << 20),
    )(side, *strips, taper_own, taper_in, *column_tables())


def row_kernel(arrived, w1h, w1l, tw, gh, gl, out, xh, xl, at, bh, bl, image, sem):
    for dl in range(4):
        for half in range(2):
            rows = jnp.swapaxes(arrived[dl, :, half * 8 : half * 8 + 8, :], 0, 1)
            for t in range(8):
                to = (half * 2 + t // 4) * 64
                lanes = (t % 4) * TILE
                high, low = split(rows[t])
                xh[dl, to : to + 64, lanes : lanes + TILE] = high
                xl[dl, to : to + 64, lanes : lanes + TILE] = low
        prod = jnp.dot(w1h[...], xh[dl], preferred_element_type=F32)
        prod += jnp.dot(w1l[...], xh[dl], preferred_element_type=F32)
        prod += jnp.dot(w1h[...], xl[dl], preferred_element_type=F32)
        at[dl] = prod

    def radix(step, carry):
        mb, block = step // 8, step % 8
        rows = pl.ds(pl.multiple_of(block * 16, 16), 16)
        rows_im = pl.ds(pl.multiple_of(TILE + block * 16, 16), 16)
        lanes = pl.ds(pl.multiple_of(mb * TILE, TILE), TILE)
        parts = [
            mul((at[dl, rows, lanes], at[dl, rows_im, lanes]), tw[dl, 0, rows, :], tw[dl, 1, rows, :])
            for dl in range(4)
        ]
        to_rows = pl.ds(pl.multiple_of(mb * TILE + block * 16, 16), 16)
        for kb, y in enumerate(dft4(*parts)):
            for p in range(2):
                high, low = split(y[p])
                bh[kb, to_rows, p * TILE : (p + 1) * TILE] = high
                bl[kb, to_rows, p * TILE : (p + 1) * TILE] = low
        return carry

    lax.fori_loop(0, 32, radix, 0, unroll=4)
    copies = []
    for half in range(2):
        rows = slice(half * 256, half * 256 + 256)
        for kb in range(4):
            prod = lax.dot_general(gh[kb], bh[kb, rows], NT, preferred_element_type=F32)
            prod += lax.dot_general(gl[kb], bh[kb, rows], NT, preferred_element_type=F32)
            prod += lax.dot_general(gh[kb], bl[kb, rows], NT, preferred_element_type=F32)
            for p in range(2):
                for k2 in range(16):
                    row = p * TILE + k2 * 8
                    to = (k2 * 4 + kb) * TILE
                    for m in range(2):
                        image[half, p, m * 8 : m * 8 + 8, to : to + TILE] = prod[
                            row : row + 8, m * TILE : (m + 1) * TILE
                        ]
        copy = pltpu.make_async_copy(
            image.at[half], out.at[:, pl.ds(half * 16, 16), :], sem.at[half]
        )
        copy.start()
        copies.append(copy)
    for copy in copies:
        copy.wait()


def row_tables():
    ka = np.arange(TILE)[:, None]
    tr, r, yh = np.meshgrid(np.arange(2), np.arange(N_ROW), np.arange(2), indexing="ij")
    coarse = (r * 4 + tr * 2 + yh).reshape(1, TILE)
    w1h, w1l = halves(real_form(*unit(TILE, ka * coarse)))
    fine = np.arange(TILE)[None, :] % 16
    turn = np.stack([np.stack(unit(G, ka * (dl * 16 + fine))) for dl in range(4)])
    k2, j = np.meshgrid(np.arange(16), np.arange(8), indexing="ij")
    k2, j = k2.reshape(TILE, 1), j.reshape(TILE, 1)
    jj, i = np.meshgrid(np.arange(8), np.arange(16), indexing="ij")
    jj, i = jj.reshape(1, TILE), i.reshape(1, TILE)
    same = (j == jj) / G
    last = []
    for kb in range(4):
        cosine, sine = unit(64, i * (kb + 4 * k2))
        last.append(real_form(cosine * same, sine * same))
    gh, gl = halves(np.stack(last))
    return w1h, w1l, turn.astype(np.float32), gh, gl


def row_call(arrived):
    vmem = pl.BlockSpec(memory_space=pltpu.VMEM)
    return pl.pallas_call(
        row_kernel,
        out_shape=jax.ShapeDtypeStruct((2, 32, G), F32),
        in_specs=[vmem, vmem, vmem, vmem, vmem, vmem],
        out_specs=pl.BlockSpec(memory_space=HBM),
        scratch_shapes=[
            pltpu.VMEM((4, 256, 512), BF16),
            pltpu.VMEM((4, 256, 512), BF16),
            pltpu.VMEM((4, 256, 512), F32),
            pltpu.VMEM((4, 512, 256), BF16),
            pltpu.VMEM((4, 512, 256), BF16),
            pltpu.VMEM((2, 2, 16, G), F32),
            pltpu.SemaphoreType.DMA((2,)),
        ],
        compiler_params=pltpu.CompilerParams(vmem_limit_bytes=40 << 20),
    )(arrived, *row_tables())


def body(visibilities, kernels, offsets, counts, slot_tiles, taper):
    me = lax.axis_index("bl")
    side = me // 4
    swap = [(s, s ^ 4) for s in range(N_BL)]
    given = lax.dynamic_slice(taper, ((1 - side) * STRIP, 0), (STRIP, G))
    taper_in = lax.ppermute(given, "bl", swap)
    strips = grid_call(
        me.reshape(1).astype(jnp.int32), counts[0], slot_tiles[0], visibilities[0, 0], kernels[0, 0], offsets[0, 0]
    )
    far, taper_in = lax.optimization_barrier((list(strips[FREE:]), taper_in))
    blocks = list(strips[:FREE]) + list(far)
    own = blocks[0] + 0.0 * me.astype(F32)
    strips = [own] + [
        lax.ppermute(blocks[i], "bl", [(s, s ^ STEPS[i]) for s in range(N_BL)])
        for i in range(1, N_BL)
    ]
    side = side.reshape(1).astype(jnp.int32)
    leaving = column_call(side, strips, taper, taper_in)
    arrived = lax.all_to_all(
        leaving.reshape(256, 16, TILE), ("bl", "row"), 0, 0, axis_index_groups=members(), tiled=True
    )
    return row_call(arrived.reshape(4, 64, 16, TILE))


def members():
    group = []
    for yl in range(2):
        for zl in range(2):
            for r in range(N_ROW):
                for yh in range(2):
                    group.append((zl * 4 + yh * 2 + yl) * N_ROW + r)
    return [group]


def solution(mesh):
    in_specs = (
        P("bl", "row", None, None, None),
        P("bl", "row", None, None, None, None),
        P("bl", "row", None, None, None),
        P("bl", "row", None),
        P("bl", "row", None),
        P(("row", "bl"), None),
    )
    out_specs = P(None, ("row", "bl"), None)
    return jax.shard_map(body, mesh=mesh, in_specs=in_specs, out_specs=out_specs, check_vma=False)
```

```python
import math

import jax
import jax.numpy as jnp
import ml_dtypes
import numpy as np
from jax import lax
from jax.experimental import pallas as pl
from jax.experimental.pallas import tpu as pltpu
from jax.sharding import PartitionSpec as P

G = 8192
TILE = 128
SUP = 8
SLOTS = 8
CAP = 768
N_BL = 8
N_ROW = 32
BANDS = 2
STRIP = TILE // N_BL
STEPS = (0, 1, 2, 3, 4, 5, 6, 7)
FREE = 6
COLS = G // TILE
F32 = jnp.float32
BF16 = jnp.bfloat16
HBM = pltpu.MemorySpace.HBM
NT = (((1,), (1,)), ((), ()))


def unit(length, phase):
    angle = 2.0 * np.pi * (np.asarray(phase, np.int64) % length) / length
    return np.cos(angle), np.sin(angle)


def real_form(cosine, sine):
    return np.block([[cosine, sine], [-sine, cosine]])


def halves(table):
    high = table.astype(ml_dtypes.bfloat16)
    low = (table - high.astype(np.float64)).astype(ml_dtypes.bfloat16)
    return high, low


def split(value):
    high = value.astype(BF16)
    low = (value - high.astype(F32)).astype(BF16)
    return high, low


def add(left, right):
    return (left[0] + right[0], left[1] + right[1])


def sub(left, right):
    return (left[0] - right[0], left[1] - right[1])


def dft4(a, b, c, d):
    s, t = add(a, c), sub(a, c)
    u, v = add(b, d), sub(b, d)
    w = (v[1], -v[0])
    return [add(s, u), add(t, w), sub(s, u), sub(t, w)]


def dft8(x):
    even = dft4(x[0], x[2], x[4], x[6])
    odd = dft4(x[1], x[3], x[5], x[7])
    r = math.sqrt(0.5)
    turned = [
        odd[0],
        ((odd[1][0] + odd[1][1]) * r, (odd[1][1] - odd[1][0]) * r),
        (odd[2][1], -odd[2][0]),
        ((odd[3][1] - odd[3][0]) * r, (odd[3][1] + odd[3][0]) * -r),
    ]
    return [add(e, o) for e, o in zip(even, turned)] + [sub(e, o) for e, o in zip(even, turned)]


def mul(x, cosine, sine):
    return (x[0] * cosine + x[1] * sine, x[1] * cosine - x[0] * sine)


def grid_kernel(
    me, counts_in, tiles_in, vis_in, taps_in, offs_in,
    out0, out1, out2, out3, out4, out5, out6, out7,
    counts, tiles, vis, taps, offs, strips, sem_few, sem_in, sem_out,
):
    outs = [out0, out1, out2, out3, out4, out5, out6, out7]
    few = [
        pltpu.make_async_copy(counts_in, counts, sem_few.at[0]),
        pltpu.make_async_copy(tiles_in, tiles, sem_few.at[1]),
        pltpu.make_async_copy(vis_in, vis, sem_few.at[2]),
        pltpu.make_async_copy(offs_in, offs, sem_few.at[3]),
    ]
    for copy in few:
        copy.start()
    tap_copies = []
    for s in range(SLOTS):
        copy = pltpu.make_async_copy(taps_in.at[s], taps.at[s], sem_in.at[s])
        copy.start()
        tap_copies.append(copy)
    for copy in few:
        copy.wait()
    sub_index = lax.broadcasted_iota(jnp.int32, (SUP, CAP), 0)
    lane = lax.broadcasted_iota(jnp.int32, (1, CAP), 1)
    slot_index = lax.broadcasted_iota(jnp.int32, (SLOTS, TILE), 0)
    numbers = jnp.zeros((SLOTS, TILE), jnp.int32)
    for s in range(SLOTS):
        numbers = jnp.where(slot_index == s, tiles[0, s], numbers)
    for block in range(N_BL):
        strips[block, 32] = numbers.astype(F32)
    leaving = []

    def place(block, taken):
        pieces = [jnp.where(taken == x, block, 0.0) for x in range(TILE // SUP)]
        return jnp.concatenate(pieces, axis=0).astype(BF16)

    def rotated(s, axis):
        first = jnp.broadcast_to(offs[s, axis : axis + 1, :], (SUP, CAP))
        shift = first & (SUP - 1)
        value = taps[s, axis]
        for bit in (1, 2, 4):
            value = jnp.where((shift & bit) != 0, pltpu.roll(value, bit, 0), value)
        taken = (first >> 3) + jnp.where(sub_index < shift, 1, 0)
        return value, taken

    for s in range(SLOTS):
        tap_copies[s].wait()
        live = lane < counts[0, s]
        value, taken = rotated(s, 0)
        lefts = [split(value * jnp.where(live, vis[s, p : p + 1, :], 0.0)) for p in range(2)]
        left = jnp.concatenate(
            [place(lefts[p][h].astype(F32), taken) for h in range(2) for p in range(2)], axis=0
        )
        value, taken = rotated(s, 1)
        rights = split(value)
        right = jnp.concatenate([place(rights[h].astype(F32), taken) for h in range(2)], axis=0)
        prod = lax.dot_general(left[:256], right, NT, preferred_element_type=F32)
        tile = prod[:, :128] + prod[:, 128:]
        tile += lax.dot_general(left[256:], right[:128], NT, preferred_element_type=F32)
        for p in range(2):
            for block in range(N_BL):
                start = p * TILE + block * STRIP
                to = s * 4 + p * 2
                strips[block, to : to + 2] = tile[start : start + STRIP].reshape(2, 8, TILE)
        if s % 4 == 3:
            part = pl.ds(s // 4 * 16, 16 + s // 7)
            for step in range(N_BL):
                other = me[0] ^ STEPS[step]
                copy = pltpu.make_async_copy(
                    strips.at[(other & 3) * 2 + (other >> 2), part],
                    outs[step].at[part],
                    sem_out.at[s // 4 * N_BL + step],
                )
                copy.start()
                leaving.append(copy)
    for copy in leaving:
        copy.wait()


def grid_call(me, counts, tiles, vis, taps, offs):
    hbm = pl.BlockSpec(memory_space=HBM)
    return pl.pallas_call(
        grid_kernel,
        out_shape=[jax.ShapeDtypeStruct((33, 8, TILE), F32)] * N_BL,
        in_specs=[pl.BlockSpec(memory_space=pltpu.SMEM)] + [hbm] * 5,
        out_specs=[pl.BlockSpec(memory_space=pltpu.VMEM)] + [hbm] * (N_BL - 1),
        scratch_shapes=[
            pltpu.SMEM((1, SLOTS), jnp.int32),
            pltpu.SMEM((1, SLOTS), jnp.int32),
            pltpu.VMEM((SLOTS, 2, CAP), F32),
            pltpu.VMEM((SLOTS, 2, SUP, CAP), F32),
            pltpu.VMEM((SLOTS, 2, CAP), jnp.int32),
            pltpu.VMEM((N_BL, 33, 8, TILE), F32),
            pltpu.SemaphoreType.DMA((4,)),
            pltpu.SemaphoreType.DMA((SLOTS,)),
            pltpu.SemaphoreType.DMA((2 * N_BL,)),
        ],
        compiler_params=pltpu.CompilerParams(vmem_limit_bytes=60 << 20),
        cost_estimate=pl.CostEstimate(flops=4 << 30, bytes_accessed=8 << 20, transcendentals=0),
    )(me, counts, tiles, vis, taps, offs)


def column_kernel(
    side, in0, in1, in2, in3, in4, in5, in6, in7, taper_own, taper_in, tw, wh, wl, out,
    taper, cells, half, xh, xl, ob, number, place, sem_in,
):
    mine = side[0]
    kept = pl.ds(pl.multiple_of(mine * STRIP, STRIP), STRIP)
    in_a = pltpu.make_async_copy(taper_own.at[kept], taper.at[mine], sem_in.at[0])
    in_b = pltpu.make_async_copy(taper_in, taper.at[1 - mine], sem_in.at[1])
    in_a.start()
    in_b.start()
    strips = [in0, in1, in2, in3, in4, in5, in6, in7]
    for block in range(N_BL):
        rows = slice(block * SLOTS, (block + 1) * SLOTS)
        number[rows, :] = strips[block][32].astype(jnp.int32)
    to_scalar = pltpu.make_async_copy(number, place, sem_in.at[2])
    to_scalar.start()
    cells[...] = jnp.zeros_like(cells)
    to_scalar.wait()

    for block in range(N_BL):
        tiles = [place[block * SLOTS + slot, 0] for slot in range(SLOTS)]
        sums = [
            cells[tile] + strips[block][slot * 4 : slot * 4 + 4] for slot, tile in enumerate(tiles)
        ]
        for tile, value in zip(tiles, sums):
            cells[tile] = value
    in_a.wait()
    in_b.wait()
    for tr in range(BANDS):
        for a0 in range(8):
            x = []
            for a1 in range(8):
                a = a1 * 8 + a0
                t = taper[tr, :, a * TILE : (a + 1) * TILE]
                z = cells[tr * COLS + a].reshape(2, STRIP, TILE)
                x.append((z[0] * t, z[1] * t))
            for k0, y in enumerate(dft8(x)):
                if a0 * k0:
                    c, s = unit(64, a0 * k0)
                    y = mul(y, float(c), float(s))
                half[k0 * 8 + a0, 0:16] = y[0]
                half[k0 * 8 + a0, 16:32] = y[1]
        for k0 in range(8):
            x = [(half[k0 * 8 + a0, 0:16], half[k0 * 8 + a0, 16:32]) for a0 in range(8)]
            for k1, y in enumerate(dft8(x)):
                k = k0 + 8 * k1
                y = mul(y, tw[0, k : k + 1, :], tw[1, k : k + 1, :])
                for p in range(2):
                    high, low = split(y[p])
                    xh[tr, k * 16 : k * 16 + 16, p * TILE : (p + 1) * TILE] = high
                    xl[tr, k * 16 : k * 16 + 16, p * TILE : (p + 1) * TILE] = low
        for block in range(4):
            rows_h = xh[tr, block * 256 : (block + 1) * 256, :]
            rows_l = xl[tr, block * 256 : (block + 1) * 256, :]
            prod = lax.dot_general(wh[...], rows_h, NT, preferred_element_type=F32)
            prod += lax.dot_general(wl[...], rows_h, NT, preferred_element_type=F32)
            prod += lax.dot_general(wh[...], rows_l, NT, preferred_element_type=F32)
            kh = block // 2
            for p in range(2):
                for m in range(2):
                    row = tr * 4 + (block % 2) * 2 + m
                    ob[kh, p, row] = prod[p * TILE : (p + 1) * TILE, m * TILE : (m + 1) * TILE]
            if tr == 1 and block % 2 == 1:
                for p in range(2):
                    out[kh, :, p * 8 : p * 8 + 8, :] = jnp.swapaxes(ob[kh, p], 0, 1)


def column_tables():
    k = np.arange(COLS)[:, None]
    y = np.arange(TILE)[None, :]
    turn = np.stack(unit(G, k * y)).astype(np.float32)
    zl, r, yh = np.meshgrid(np.arange(2), np.arange(N_ROW), np.arange(2), indexing="ij")
    q = (r * 4 + zl * 2 + yh).reshape(TILE, 1)
    high, low = halves(real_form(*unit(TILE, q * y)))
    return turn, high, low


def column_call(side, strips, taper_own, taper_in):
    smem = pl.BlockSpec(memory_space=pltpu.SMEM)
    vmem = pl.BlockSpec(memory_space=pltpu.VMEM)
    hbm = pl.BlockSpec(memory_space=pl.ANY)
    return pl.pallas_call(
        column_kernel,
        out_shape=jax.ShapeDtypeStruct((2, TILE, 16, TILE), F32),
        in_specs=[smem] + [vmem] * N_BL + [hbm, hbm, vmem, vmem, vmem],
        out_specs=vmem,
        scratch_shapes=[
            pltpu.VMEM((2, STRIP, G), F32),
            pltpu.VMEM((BANDS * COLS, 4, 8, TILE), F32),
            pltpu.VMEM((64, 32, TILE), F32),
            pltpu.VMEM((BANDS, 1024, 256), BF16),
            pltpu.VMEM((BANDS, 1024, 256), BF16),
            pltpu.VMEM((2, 2, 8, TILE, TILE), F32),
            pltpu.VMEM((64, TILE), jnp.int32),
            pltpu.SMEM((64, TILE), jnp.int32),
            pltpu.SemaphoreType.DMA((3,)),
        ],
        compiler_params=pltpu.CompilerParams(vmem_limit_bytes=40 << 20),
    )(side, *strips, taper_own, taper_in, *column_tables())


def row_kernel(arrived, w1h, w1l, tw, gh, gl, out, xh, xl, at, bh, bl, image, sem):
    for dl in range(4):
        for half in range(2):
            rows = jnp.swapaxes(arrived[dl, :, half * 8 : half * 8 + 8, :], 0, 1)
            for t in range(8):
                to = (half * 2 + t // 4) * 64
                lanes = (t % 4) * TILE
                high, low = split(rows[t])
                xh[dl, to : to + 64, lanes : lanes + TILE] = high
                xl[dl, to : to + 64, lanes : lanes + TILE] = low
        prod = jnp.dot(w1h[...], xh[dl], preferred_element_type=F32)
        prod += jnp.dot(w1l[...], xh[dl], preferred_element_type=F32)
        prod += jnp.dot(w1h[...], xl[dl], preferred_element_type=F32)
        at[dl] = prod

    def radix(step, carry):
        mb, block = step // 8, step % 8
        rows = pl.ds(pl.multiple_of(block * 16, 16), 16)
        rows_im = pl.ds(pl.multiple_of(TILE + block * 16, 16), 16)
        lanes = pl.ds(pl.multiple_of(mb * TILE, TILE), TILE)
        parts = [
            mul((at[dl, rows, lanes], at[dl, rows_im, lanes]), tw[dl, 0, rows, :], tw[dl, 1, rows, :])
            for dl in range(4)
        ]
        to_rows = pl.ds(pl.multiple_of(mb * TILE + block * 16, 16), 16)
        for kb, y in enumerate(dft4(*parts)):
            for p in range(2):
                high, low = split(y[p])
                bh[kb, to_rows, p * TILE : (p + 1) * TILE] = high
                bl[kb, to_rows, p * TILE : (p + 1) * TILE] = low
        return carry

    copies = []
    for half in range(2):
        lax.fori_loop(half * 16, half * 16 + 16, radix, 0, unroll=8)
        rows = slice(half * 256, half * 256 + 256)
        for kb in range(4):
            prod = lax.dot_general(gh[kb], bh[kb, rows], NT, preferred_element_type=F32)
            prod += lax.dot_general(gl[kb], bh[kb, rows], NT, preferred_element_type=F32)
            prod += lax.dot_general(gh[kb], bl[kb, rows], NT, preferred_element_type=F32)
            for p in range(2):
                for k2 in range(16):
                    row = p * TILE + k2 * 8
                    to = (k2 * 4 + kb) * TILE
                    for m in range(2):
                        image[half, p, m * 8 : m * 8 + 8, to : to + TILE] = prod[
                            row : row + 8, m * TILE : (m + 1) * TILE
                        ]
        copy = pltpu.make_async_copy(
            image.at[half], out.at[:, pl.ds(half * 16, 16), :], sem.at[half]
        )
        copy.start()
        copies.append(copy)
    for copy in copies:
        copy.wait()


def row_tables():
    ka = np.arange(TILE)[:, None]
    tr, r, yh = np.meshgrid(np.arange(2), np.arange(N_ROW), np.arange(2), indexing="ij")
    coarse = (r * 4 + tr * 2 + yh).reshape(1, TILE)
    w1h, w1l = halves(real_form(*unit(TILE, ka * coarse)))
    fine = np.arange(TILE)[None, :] % 16
    turn = np.stack([np.stack(unit(G, ka * (dl * 16 + fine))) for dl in range(4)])
    k2, j = np.meshgrid(np.arange(16), np.arange(8), indexing="ij")
    k2, j = k2.reshape(TILE, 1), j.reshape(TILE, 1)
    jj, i = np.meshgrid(np.arange(8), np.arange(16), indexing="ij")
    jj, i = jj.reshape(1, TILE), i.reshape(1, TILE)
    same = (j == jj) / G
    last = []
    for kb in range(4):
        cosine, sine = unit(64, i * (kb + 4 * k2))
        last.append(real_form(cosine * same, sine * same))
    gh, gl = halves(np.stack(last))
    return w1h, w1l, turn.astype(np.float32), gh, gl


def row_call(arrived):
    vmem = pl.BlockSpec(memory_space=pltpu.VMEM)
    return pl.pallas_call(
        row_kernel,
        out_shape=jax.ShapeDtypeStruct((2, 32, G), F32),
        in_specs=[vmem, vmem, vmem, vmem, vmem, vmem],
        out_specs=pl.BlockSpec(memory_space=HBM),
        scratch_shapes=[
            pltpu.VMEM((4, 256, 512), BF16),
            pltpu.VMEM((4, 256, 512), BF16),
            pltpu.VMEM((4, 256, 512), F32),
            pltpu.VMEM((4, 512, 256), BF16),
            pltpu.VMEM((4, 512, 256), BF16),
            pltpu.VMEM((2, 2, 16, G), F32),
            pltpu.SemaphoreType.DMA((2,)),
        ],
        compiler_params=pltpu.CompilerParams(vmem_limit_bytes=40 << 20),
    )(arrived, *row_tables())


def body(visibilities, kernels, offsets, counts, slot_tiles, taper):
    me = lax.axis_index("bl")
    side = me // 4
    swap = [(s, s ^ 4) for s in range(N_BL)]
    given = lax.dynamic_slice(taper, ((1 - side) * STRIP, 0), (STRIP, G))
    taper_in = lax.ppermute(given, "bl", swap)
    strips = grid_call(
        me.reshape(1).astype(jnp.int32), counts[0], slot_tiles[0], visibilities[0, 0], kernels[0, 0], offsets[0, 0]
    )
    far, taper_in = lax.optimization_barrier((list(strips[FREE:]), taper_in))
    blocks = list(strips[:FREE]) + list(far)
    own = blocks[0] + 0.0 * me.astype(F32)
    strips = [own] + [
        lax.ppermute(blocks[i], "bl", [(s, s ^ STEPS[i]) for s in range(N_BL)])
        for i in range(1, N_BL)
    ]
    side = side.reshape(1).astype(jnp.int32)
    leaving = column_call(side, strips, taper, taper_in)
    arrived = lax.all_to_all(
        leaving.reshape(256, 16, TILE), ("bl", "row"), 0, 0, axis_index_groups=members(), tiled=True
    )
    return row_call(arrived.reshape(4, 64, 16, TILE))


def members():
    group = []
    for yl in range(2):
        for zl in range(2):
            for r in range(N_ROW):
                for yh in range(2):
                    group.append((zl * 4 + yh * 2 + yl) * N_ROW + r)
    return [group]


def solution(mesh):
    in_specs = (
        P("bl", "row", None, None, None),
        P("bl", "row", None, None, None, None),
        P("bl", "row", None, None, None),
        P("bl", "row", None),
        P("bl", "row", None),
        P(("row", "bl"), None),
    )
    out_specs = P(None, ("row", "bl"), None)
    return jax.shard_map(body, mesh=mesh, in_specs=in_specs, out_specs=out_specs, check_vma=False)
```

```python
import math

import jax
import jax.numpy as jnp
import ml_dtypes
import numpy as np
from jax import lax
from jax.experimental import pallas as pl
from jax.experimental.pallas import tpu as pltpu
from jax.sharding import PartitionSpec as P

G = 8192
TILE = 128
SUP = 8
SLOTS = 8
CAP = 768
N_BL = 8
N_ROW = 32
BANDS = 2
STRIP = TILE // N_BL
STEPS = (0, 1, 2, 3, 4, 5, 6, 7)
FREE = 6
COLS = G // TILE
F32 = jnp.float32
BF16 = jnp.bfloat16
HBM = pltpu.MemorySpace.HBM
NT = (((1,), (1,)), ((), ()))


def unit(length, phase):
    angle = 2.0 * np.pi * (np.asarray(phase, np.int64) % length) / length
    return np.cos(angle), np.sin(angle)


def real_form(cosine, sine):
    return np.block([[cosine, sine], [-sine, cosine]])


def halves(table):
    high = table.astype(ml_dtypes.bfloat16)
    low = (table - high.astype(np.float64)).astype(ml_dtypes.bfloat16)
    return high, low


def split(value):
    high = value.astype(BF16)
    low = (value - high.astype(F32)).astype(BF16)
    return high, low


def add(left, right):
    return (left[0] + right[0], left[1] + right[1])


def sub(left, right):
    return (left[0] - right[0], left[1] - right[1])


def dft4(a, b, c, d):
    s, t = add(a, c), sub(a, c)
    u, v = add(b, d), sub(b, d)
    w = (v[1], -v[0])
    return [add(s, u), add(t, w), sub(s, u), sub(t, w)]


def dft8(x):
    even = dft4(x[0], x[2], x[4], x[6])
    odd = dft4(x[1], x[3], x[5], x[7])
    r = math.sqrt(0.5)
    turned = [
        odd[0],
        ((odd[1][0] + odd[1][1]) * r, (odd[1][1] - odd[1][0]) * r),
        (odd[2][1], -odd[2][0]),
        ((odd[3][1] - odd[3][0]) * r, (odd[3][1] + odd[3][0]) * -r),
    ]
    return [add(e, o) for e, o in zip(even, turned)] + [sub(e, o) for e, o in zip(even, turned)]


def mul(x, cosine, sine):
    return (x[0] * cosine + x[1] * sine, x[1] * cosine - x[0] * sine)


def grid_kernel(
    me, counts_in, tiles_in, vis_in, taps_in, offs_in,
    out0, out1, out2, out3, out4, out5, out6, out7,
    counts, tiles, vis, taps, offs, strips, sem_few, sem_in, sem_out,
):
    outs = [out0, out1, out2, out3, out4, out5, out6, out7]
    few = [
        pltpu.make_async_copy(counts_in, counts, sem_few.at[0]),
        pltpu.make_async_copy(tiles_in, tiles, sem_few.at[1]),
        pltpu.make_async_copy(vis_in, vis, sem_few.at[2]),
        pltpu.make_async_copy(offs_in, offs, sem_few.at[3]),
    ]
    for copy in few:
        copy.start()
    tap_copies = []
    for s in range(SLOTS):
        copy = pltpu.make_async_copy(taps_in.at[s], taps.at[s], sem_in.at[s])
        copy.start()
        tap_copies.append(copy)
    for copy in few:
        copy.wait()
    sub_index = lax.broadcasted_iota(jnp.int32, (SUP, CAP), 0)
    lane = lax.broadcasted_iota(jnp.int32, (1, CAP), 1)
    slot_index = lax.broadcasted_iota(jnp.int32, (SLOTS, TILE), 0)
    numbers = jnp.zeros((SLOTS, TILE), jnp.int32)
    for s in range(SLOTS):
        numbers = jnp.where(slot_index == s, tiles[0, s], numbers)
    for block in range(N_BL):
        strips[block, 32] = numbers.astype(F32)
    leaving = []

    def place(block, taken):
        pieces = [jnp.where(taken == x, block, 0.0) for x in range(TILE // SUP)]
        return jnp.concatenate(pieces, axis=0).astype(BF16)

    def rotated(s, axis):
        first = jnp.broadcast_to(offs[s, axis : axis + 1, :], (SUP, CAP))
        shift = first & (SUP - 1)
        value = taps[s, axis]
        for bit in (1, 2, 4):
            value = jnp.where((shift & bit) != 0, pltpu.roll(value, bit, 0), value)
        taken = (first >> 3) + jnp.where(sub_index < shift, 1, 0)
        return value, taken

    for s in range(SLOTS):
        tap_copies[s].wait()
        live = lane < counts[0, s]
        value, taken = rotated(s, 0)
        lefts = [split(value * jnp.where(live, vis[s, p : p + 1, :], 0.0)) for p in range(2)]
        left = jnp.concatenate(
            [place(lefts[p][h].astype(F32), taken) for h in range(2) for p in range(2)], axis=0
        )
        value, taken = rotated(s, 1)
        rights = split(value)
        right = jnp.concatenate([place(rights[h].astype(F32), taken) for h in range(2)], axis=0)
        prod = lax.dot_general(left[:256], right, NT, preferred_element_type=F32)
        tile = prod[:, :128] + prod[:, 128:]
        tile += lax.dot_general(left[256:], right[:128], NT, preferred_element_type=F32)
        for p in range(2):
            for block in range(N_BL):
                start = p * TILE + block * STRIP
                to = s * 4 + p * 2
                strips[block, to : to + 2] = tile[start : start + STRIP].reshape(2, 8, TILE)
        if s % 4 == 3:
            part = pl.ds(s // 4 * 16, 16 + s // 7)
            for step in range(N_BL):
                other = me[0] ^ STEPS[step]
                copy = pltpu.make_async_copy(
                    strips.at[(other & 3) * 2 + (other >> 2), part],
                    outs[step].at[part],
                    sem_out.at[s // 4 * N_BL + step],
                )
                copy.start()
                leaving.append(copy)
    for copy in leaving:
        copy.wait()


def grid_call(me, counts, tiles, vis, taps, offs):
    hbm = pl.BlockSpec(memory_space=HBM)
    return pl.pallas_call(
        grid_kernel,
        out_shape=[jax.ShapeDtypeStruct((33, 8, TILE), F32)] * N_BL,
        in_specs=[pl.BlockSpec(memory_space=pltpu.SMEM)] + [hbm] * 5,
        out_specs=[pl.BlockSpec(memory_space=pltpu.VMEM)] + [hbm] * (N_BL - 1),
        scratch_shapes=[
            pltpu.SMEM((1, SLOTS), jnp.int32),
            pltpu.SMEM((1, SLOTS), jnp.int32),
            pltpu.VMEM((SLOTS, 2, CAP), F32),
            pltpu.VMEM((SLOTS, 2, SUP, CAP), F32),
            pltpu.VMEM((SLOTS, 2, CAP), jnp.int32),
            pltpu.VMEM((N_BL, 33, 8, TILE), F32),
            pltpu.SemaphoreType.DMA((4,)),
            pltpu.SemaphoreType.DMA((SLOTS,)),
            pltpu.SemaphoreType.DMA((2 * N_BL,)),
        ],
        compiler_params=pltpu.CompilerParams(vmem_limit_bytes=60 << 20),
        cost_estimate=pl.CostEstimate(flops=4 << 30, bytes_accessed=8 << 20, transcendentals=0),
    )(me, counts, tiles, vis, taps, offs)


def column_kernel(
    side, in0, in1, in2, in3, in4, in5, in6, in7, taper_own, taper_in, tw, wh, wl, out,
    taper, cells, half, xh, xl, ob, number, place, sem_in,
):
    mine = side[0]
    kept = pl.ds(pl.multiple_of(mine * STRIP, STRIP), STRIP)
    in_a = pltpu.make_async_copy(taper_own.at[kept], taper.at[mine], sem_in.at[0])
    in_b = pltpu.make_async_copy(taper_in, taper.at[1 - mine], sem_in.at[1])
    in_a.start()
    in_b.start()
    strips = [in0, in1, in2, in3, in4, in5, in6, in7]
    for block in range(N_BL):
        rows = slice(block * SLOTS, (block + 1) * SLOTS)
        number[rows, :] = strips[block][32].astype(jnp.int32)
    to_scalar = pltpu.make_async_copy(number, place, sem_in.at[2])
    to_scalar.start()
    cells[...] = jnp.zeros_like(cells)
    to_scalar.wait()

    for block in range(N_BL):
        tiles = [place[block * SLOTS + slot, 0] for slot in range(SLOTS)]
        sums = [
            cells[tile] + strips[block][slot * 4 : slot * 4 + 4] for slot, tile in enumerate(tiles)
        ]
        for tile, value in zip(tiles, sums):
            cells[tile] = value
    in_a.wait()
    in_b.wait()
    for tr in range(BANDS):
        for a0 in range(8):
            x = []
            for a1 in range(8):
                a = a1 * 8 + a0
                t = taper[tr, :, a * TILE : (a + 1) * TILE]
                z = cells[tr * COLS + a].reshape(2, STRIP, TILE)
                x.append((z[0] * t, z[1] * t))
            for k0, y in enumerate(dft8(x)):
                if a0 * k0:
                    c, s = unit(64, a0 * k0)
                    y = mul(y, float(c), float(s))
                half[k0 * 8 + a0, 0:16] = y[0]
                half[k0 * 8 + a0, 16:32] = y[1]
        for k0 in range(8):
            x = [(half[k0 * 8 + a0, 0:16], half[k0 * 8 + a0, 16:32]) for a0 in range(8)]
            for k1, y in enumerate(dft8(x)):
                k = k0 + 8 * k1
                y = mul(y, tw[0, k : k + 1, :], tw[1, k : k + 1, :])
                for p in range(2):
                    high, low = split(y[p])
                    xh[tr, k * 16 : k * 16 + 16, p * TILE : (p + 1) * TILE] = high
                    xl[tr, k * 16 : k * 16 + 16, p * TILE : (p + 1) * TILE] = low
        for block in range(4):
            rows_h = xh[tr, block * 256 : (block + 1) * 256, :]
            rows_l = xl[tr, block * 256 : (block + 1) * 256, :]
            prod = lax.dot_general(wh[...], rows_h, NT, preferred_element_type=F32)
            prod += lax.dot_general(wl[...], rows_h, NT, preferred_element_type=F32)
            prod += lax.dot_general(wh[...], rows_l, NT, preferred_element_type=F32)
            kh = block // 2
            for p in range(2):
                for m in range(2):
                    row = tr * 4 + (block % 2) * 2 + m
                    ob[kh, p, row] = prod[p * TILE : (p + 1) * TILE, m * TILE : (m + 1) * TILE]
            if tr == 1 and block % 2 == 1:
                for p in range(2):
                    out[kh, :, p * 8 : p * 8 + 8, :] = jnp.swapaxes(ob[kh, p], 0, 1)


def column_tables():
    k = np.arange(COLS)[:, None]
    y = np.arange(TILE)[None, :]
    turn = np.stack(unit(G, k * y)).astype(np.float32)
    zl, r, yh = np.meshgrid(np.arange(2), np.arange(N_ROW), np.arange(2), indexing="ij")
    q = (r * 4 + zl * 2 + yh).reshape(TILE, 1)
    high, low = halves(real_form(*unit(TILE, q * y)))
    return turn, high, low


def column_call(side, strips, taper_own, taper_in):
    smem = pl.BlockSpec(memory_space=pltpu.SMEM)
    vmem = pl.BlockSpec(memory_space=pltpu.VMEM)
    hbm = pl.BlockSpec(memory_space=pl.ANY)
    return pl.pallas_call(
        column_kernel,
        out_shape=jax.ShapeDtypeStruct((2, TILE, 16, TILE), F32),
        in_specs=[smem] + [vmem] * N_BL + [hbm, hbm, vmem, vmem, vmem],
        out_specs=vmem,
        scratch_shapes=[
            pltpu.VMEM((2, STRIP, G), F32),
            pltpu.VMEM((BANDS * COLS, 4, 8, TILE), F32),
            pltpu.VMEM((64, 32, TILE), F32),
            pltpu.VMEM((BANDS, 1024, 256), BF16),
            pltpu.VMEM((BANDS, 1024, 256), BF16),
            pltpu.VMEM((2, 2, 8, TILE, TILE), F32),
            pltpu.VMEM((64, TILE), jnp.int32),
            pltpu.SMEM((64, TILE), jnp.int32),
            pltpu.SemaphoreType.DMA((3,)),
        ],
        compiler_params=pltpu.CompilerParams(vmem_limit_bytes=40 << 20),
    )(side, *strips, taper_own, taper_in, *column_tables())


def row_kernel(arrived, w1h, w1l, tw, gh, gl, out, xh, xl, at, bh, bl, image, sem):
    for dl in range(4):
        for half in range(2):
            rows = jnp.swapaxes(arrived[dl, :, half * 8 : half * 8 + 8, :], 0, 1)
            for t in range(8):
                to = (half * 2 + t // 4) * 64
                lanes = (t % 4) * TILE
                high, low = split(rows[t])
                xh[dl, to : to + 64, lanes : lanes + TILE] = high
                xl[dl, to : to + 64, lanes : lanes + TILE] = low
        prod = jnp.dot(w1h[...], xh[dl], preferred_element_type=F32)
        prod += jnp.dot(w1l[...], xh[dl], preferred_element_type=F32)
        prod += jnp.dot(w1h[...], xl[dl], preferred_element_type=F32)
        at[dl] = prod

    def radix(step, carry):
        mb, block = step // 8, step % 8
        rows = pl.ds(pl.multiple_of(block * 16, 16), 16)
        rows_im = pl.ds(pl.multiple_of(TILE + block * 16, 16), 16)
        lanes = pl.ds(pl.multiple_of(mb * TILE, TILE), TILE)
        parts = [
            mul((at[dl, rows, lanes], at[dl, rows_im, lanes]), tw[dl, 0, rows, :], tw[dl, 1, rows, :])
            for dl in range(4)
        ]
        to_rows = pl.ds(pl.multiple_of(mb * TILE + block * 16, 16), 16)
        for kb, y in enumerate(dft4(*parts)):
            for p in range(2):
                high, low = split(y[p])
                bh[kb, to_rows, p * TILE : (p + 1) * TILE] = high
                bl[kb, to_rows, p * TILE : (p + 1) * TILE] = low
        return carry

    copies = []
    for half in range(2):
        lax.fori_loop(half * 16, half * 16 + 16, radix, 0, unroll=2)
        rows = slice(half * 256, half * 256 + 256)
        for kb in range(4):
            prod = lax.dot_general(gh[kb], bh[kb, rows], NT, preferred_element_type=F32)
            prod += lax.dot_general(gl[kb], bh[kb, rows], NT, preferred_element_type=F32)
            prod += lax.dot_general(gh[kb], bl[kb, rows], NT, preferred_element_type=F32)
            for p in range(2):
                for k2 in range(16):
                    row = p * TILE + k2 * 8
                    to = (k2 * 4 + kb) * TILE
                    for m in range(2):
                        image[half, p, m * 8 : m * 8 + 8, to : to + TILE] = prod[
                            row : row + 8, m * TILE : (m + 1) * TILE
                        ]
        copy = pltpu.make_async_copy(
            image.at[half], out.at[:, pl.ds(half * 16, 16), :], sem.at[half]
        )
        copy.start()
        copies.append(copy)
    for copy in copies:
        copy.wait()


def row_tables():
    ka = np.arange(TILE)[:, None]
    tr, r, yh = np.meshgrid(np.arange(2), np.arange(N_ROW), np.arange(2), indexing="ij")
    coarse = (r * 4 + tr * 2 + yh).reshape(1, TILE)
    w1h, w1l = halves(real_form(*unit(TILE, ka * coarse)))
    fine = np.arange(TILE)[None, :] % 16
    turn = np.stack([np.stack(unit(G, ka * (dl * 16 + fine))) for dl in range(4)])
    k2, j = np.meshgrid(np.arange(16), np.arange(8), indexing="ij")
    k2, j = k2.reshape(TILE, 1), j.reshape(TILE, 1)
    jj, i = np.meshgrid(np.arange(8), np.arange(16), indexing="ij")
    jj, i = jj.reshape(1, TILE), i.reshape(1, TILE)
    same = (j == jj) / G
    last = []
    for kb in range(4):
        cosine, sine = unit(64, i * (kb + 4 * k2))
        last.append(real_form(cosine * same, sine * same))
    gh, gl = halves(np.stack(last))
    return w1h, w1l, turn.astype(np.float32), gh, gl


def row_call(arrived):
    vmem = pl.BlockSpec(memory_space=pltpu.VMEM)
    return pl.pallas_call(
        row_kernel,
        out_shape=jax.ShapeDtypeStruct((2, 32, G), F32),
        in_specs=[vmem, vmem, vmem, vmem, vmem, vmem],
        out_specs=pl.BlockSpec(memory_space=HBM),
        scratch_shapes=[
            pltpu.VMEM((4, 256, 512), BF16),
            pltpu.VMEM((4, 256, 512), BF16),
            pltpu.VMEM((4, 256, 512), F32),
            pltpu.VMEM((4, 512, 256), BF16),
            pltpu.VMEM((4, 512, 256), BF16),
            pltpu.VMEM((2, 2, 16, G), F32),
            pltpu.SemaphoreType.DMA((2,)),
        ],
        compiler_params=pltpu.CompilerParams(vmem_limit_bytes=40 << 20),
    )(arrived, *row_tables())


def body(visibilities, kernels, offsets, counts, slot_tiles, taper):
    me = lax.axis_index("bl")
    side = me // 4
    swap = [(s, s ^ 4) for s in range(N_BL)]
    given = lax.dynamic_slice(taper, ((1 - side) * STRIP, 0), (STRIP, G))
    taper_in = lax.ppermute(given, "bl", swap)
    strips = grid_call(
        me.reshape(1).astype(jnp.int32), counts[0], slot_tiles[0], visibilities[0, 0], kernels[0, 0], offsets[0, 0]
    )
    far, taper_in = lax.optimization_barrier((list(strips[FREE:]), taper_in))
    blocks = list(strips[:FREE]) + list(far)
    own = blocks[0] + 0.0 * me.astype(F32)
    strips = [own] + [
        lax.ppermute(blocks[i], "bl", [(s, s ^ STEPS[i]) for s in range(N_BL)])
        for i in range(1, N_BL)
    ]
    side = side.reshape(1).astype(jnp.int32)
    leaving = column_call(side, strips, taper, taper_in)
    arrived = lax.all_to_all(
        leaving.reshape(256, 16, TILE), ("bl", "row"), 0, 0, axis_index_groups=members(), tiled=True
    )
    return row_call(arrived.reshape(4, 64, 16, TILE))


def members():
    group = []
    for yl in range(2):
        for zl in range(2):
            for r in range(N_ROW):
                for yh in range(2):
                    group.append((zl * 4 + yh * 2 + yl) * N_ROW + r)
    return [group]


def solution(mesh):
    in_specs = (
        P("bl", "row", None, None, None),
        P("bl", "row", None, None, None, None),
        P("bl", "row", None, None, None),
        P("bl", "row", None),
        P("bl", "row", None),
        P(("row", "bl"), None),
    )
    out_specs = P(None, ("row", "bl"), None)
    return jax.shard_map(body, mesh=mesh, in_specs=in_specs, out_specs=out_specs, check_vma=False)
```
